32 devices in a mesh: section: 2 (over core), dp: 4 (over z), rep: 4 (over y, x).
Axes of the slice: x: 2, y: 2, z: 4, core: 2. Of those that a mesh axis runs over, the one named last changes fastest.
Arguments:
- inputs: bfloat16 [2, 8192, 768], P(None, ('dp', 'rep')), may hold values from -1.6953125 to 1.6953125
- segments: int32 [2, 8192], P(None, ('dp', 'rep')), may hold values from 0 to 8, as said below
- cotangent: bfloat16 [2, 8192, 768], P(None, ('dp', 'rep')), may hold values from -6 to 6
- w_qkv: bfloat16 [2, 768, 2304], P('section'), may hold values from -1 to 1
- b_qkv: bfloat16 [2, 2304], P('section'), may hold values from -0.796875 to 0.796875
- w_out: bfloat16 [2, 768, 768], P('section'), may hold values from -0.875 to 0.875
- b_out: bfloat16 [2, 768], P('section'), may hold values from -0.5 to 0.5
- g_attn: bfloat16 [2, 768], P('section'), may hold values from 0.5 to 1.5
- b_attn: bfloat16 [2, 768], P('section'), may hold values from -0.5 to 0.5
- w_in: bfloat16 [2, 768, 3072], P('section'), may hold values from -0.21875 to 0.21875
- b_in: bfloat16 [2, 3072], P('section'), may hold values from -0.796875 to 0.796875
- w_down: bfloat16 [2, 3072, 768], P('section'), may hold values from -0.15625 to 0.15625
- b_down: bfloat16 [2, 768], P('section'), may hold values from -0.5 to 0.5
- g_ffn: bfloat16 [2, 768], P('section'), may hold values from 0.5 to 1.5
- b_ffn: bfloat16 [2, 768], P('section'), may hold values from -0.5 to 0.5
Outputs:
- acts: bfloat16 [2, 2, 8192, 768], P('section', None, ('dp', 'rep'))
- in_grads: bfloat16 [2, 2, 8192, 768], P('section', None, ('dp', 'rep'))
- grad_w_qkv: float32 [2, 768, 2304], P('section')
- grad_b_qkv: float32 [2, 2304], P('section')
- grad_w_out: float32 [2, 768, 768], P('section')
- grad_b_out: float32 [2, 768], P('section')
- grad_g_attn: float32 [2, 768], P('section')
- grad_b_attn: float32 [2, 768], P('section')
- grad_w_in: float32 [2, 768, 3072], P('section')
- grad_b_in: float32 [2, 3072], P('section')
- grad_w_down: float32 [2, 3072, 768], P('section')
- grad_b_down: float32 [2, 768], P('section')
- grad_g_ffn: float32 [2, 768], P('section')
- grad_b_ffn: float32 [2, 768], P('section')
The draws below stay inside these ranges and needn't reach their ends.
Inputs may be any that keep to these rules, and one draw needn't show every extreme that they name: `segments`: in every aligned run of 512 tokens of one micro-batch the live tokens come first and form whole sequences numbered 0, 1, 2, ... in order, each a multiple of 64 tokens long; the rest of the run is padding, marked 512 // 64. Some run is one sequence of all 512 tokens, and some run holds padding.
All inputs are finite; a program needn't handle non-finite values.
Results may differ from the reference program's by a relative error of at most 0.015.
Values may be sent and summed in bfloat16 or wider, within the bound.
A program may use at most 320 MiB of HBM per device.

```python
import math
import jax
import jax.numpy as jnp
from jax import lax

D = 768
HEADS = 12
HEAD = 64
FF = 3072
SLOT = 512
MINLEN = 64
MICRO = 2
TOKENS = 8192
N_SECTION = 2


def draw_segments(key, part):
    key = jax.random.fold_in(key, 7)
    run_count = MICRO * TOKENS // SLOT
    blocks = SLOT // MINLEN
    keys_all = jax.random.split(key, 4)
    shrink = jax.random.randint(keys_all[0], (run_count,), 0, 3).astype(jnp.int32)
    live_blocks = jnp.maximum(jnp.right_shift(jnp.full((run_count,), blocks, jnp.int32), shrink), 1)
    full_run = jax.random.randint(keys_all[1], (), 0, run_count).astype(jnp.int32)
    half_run = (full_run + 1 + jax.random.randint(keys_all[2], (), 0, run_count - 1).astype(jnp.int32)) % run_count
    run_ids = jnp.arange(run_count).astype(jnp.int32)
    live_blocks = jnp.where(run_ids == full_run, blocks, live_blocks)
    live_blocks = jnp.where(run_ids == half_run, blocks // 2, live_blocks)
    block_ids = jnp.arange(blocks).astype(jnp.int32)
    starts = jax.random.randint(keys_all[3], (run_count, blocks), 0, 3) == 0
    starts = starts | (block_ids[None, :] == 0)
    starts = jnp.where((run_ids == full_run)[:, None], block_ids[None, :] == 0, starts)
    numbers = jnp.cumsum(starts.astype(jnp.int32), axis=1).astype(jnp.int32) - 1
    numbers = jnp.where(block_ids[None, :] < live_blocks[:, None], numbers, blocks)
    return jnp.repeat(numbers, MINLEN, axis=1).reshape(MICRO, TOKENS).astype(jnp.int32)


def draw_w_qkv(key, part):
    key = jax.random.fold_in(key, 11)
    bound = math.sqrt(3.0 / D)
    unit = jax.random.uniform(key, (N_SECTION, D, 3 * D), jnp.float32, -1.0, 1.0)
    return (unit * bound).astype(jnp.bfloat16)


def strengthened(entries, own_key, source, target, parts, factor):
    owner, partner = [(jnp.arange(entries.shape[dim]) // (entries.shape[dim] // parts)).reshape([-1 if axis == dim else 1 for axis in range(entries.ndim)]) for dim in (source, target)]
    chosen = jax.random.permutation(own_key, parts)[partner]
    strong = (owner == chosen) | (owner == (partner + parts // 2) % parts)
    return jnp.where(strong, factor * entries, entries)


def shard_levels(own_key, shape, shards, smallest, high):
    loudness = 1.0
    for dim, shards_of in shards:
        draws = jax.random.uniform(jax.random.fold_in(jax.random.fold_in(own_key, 6), dim), (shards_of,), jnp.float32, smallest / len(shards), high / len(shards))
        loudness = loudness * jnp.repeat(jnp.exp(draws), shape[dim] // shards_of).reshape((-1,) + (1,) * (len(shape) - 1 - dim))
    return loudness


def bell_draw(stream_key, extent, scale, limit, cuts=(), kind=jnp.bfloat16):
    loudness = shard_levels(stream_key, extent, cuts, -0.22, 0.18) if cuts else 1.0
    drawn = jax.random.normal(stream_key, extent, jnp.float32) * scale * loudness
    return jnp.minimum(jnp.maximum(drawn, -limit), limit).astype(kind)


def gaussian_with(key, extent, scale, reach, cuts, heavy, held_as=jnp.bfloat16):
    values = scale * jax.random.normal(key, extent, jnp.float32)
    if cuts:
        values = values * shard_levels(key, extent, cuts, -0.22, 0.18)
    return jnp.clip(strengthened(values, jax.random.fold_in(key, 3), *heavy), -reach, reach).astype(held_as)


def setup_inputs(seed: int = 0) -> dict:
    keys = jax.random.split(jax.random.key(seed), 16)
    return {
        "inputs": jnp.clip(jax.random.uniform(keys[0], (MICRO, TOKENS, D), jnp.float32, -1.6953125, 1.6953125) * shard_levels(keys[0], (MICRO, TOKENS, D), ((1, 16),), -0.4, 0.0), -1.6953125, 1.6953125).astype(jnp.bfloat16),
        "segments": draw_segments(jax.random.fold_in(keys[15], 71), 0),
        "cotangent": gaussian_with(keys[2], (MICRO, TOKENS, D), 1.0, 6.0, ((1, 16),), (1, 2, 16, 2.0)),
        "w_qkv": draw_w_qkv(jax.random.fold_in(keys[15], 71), 0),
        "b_qkv": jnp.clip(jax.random.uniform(keys[4], (N_SECTION, 3 * D), jnp.float32, -0.796875, 0.796875) * shard_levels(keys[4], (N_SECTION, 3 * D), ((0, 2),), -0.4, 0.0), -0.796875, 0.796875).astype(jnp.bfloat16),
        "w_out": bell_draw(keys[5], (N_SECTION, D, D), (D // 16) ** -0.5, 0.875, ((0, 2),)),
        "b_out": jnp.clip(jax.random.uniform(keys[6], (N_SECTION, D), jnp.float32, -0.5, 0.5) * shard_levels(keys[6], (N_SECTION, D), ((0, 2),), -0.4, 0.0), -0.5, 0.5).astype(jnp.bfloat16),
        "g_attn": jnp.clip(1.0 + 0.1 * jax.random.normal(keys[7], (N_SECTION, D), jnp.float32), 0.5, 1.5).astype(jnp.bfloat16),
        "b_attn": jnp.clip(jax.random.uniform(keys[8], (N_SECTION, D), jnp.float32, -0.5, 0.5) * shard_levels(keys[8], (N_SECTION, D), ((0, 2),), -0.4, 0.0), -0.5, 0.5).astype(jnp.bfloat16),
        "w_in": bell_draw(keys[9], (N_SECTION, D, FF), D ** -0.5, 0.21875, ((0, 2),)),
        "b_in": jnp.clip(jax.random.uniform(keys[10], (N_SECTION, FF), jnp.float32, -0.796875, 0.796875) * shard_levels(keys[10], (N_SECTION, FF), ((0, 2),), -0.4, 0.0), -0.796875, 0.796875).astype(jnp.bfloat16),
        "w_down": bell_draw(keys[11], (N_SECTION, FF, D), (FF // 2) ** -0.5, 0.15625, ((0, 2),)),
        "b_down": jnp.clip(jax.random.uniform(keys[12], (N_SECTION, D), jnp.float32, -0.5, 0.5) * shard_levels(keys[12], (N_SECTION, D), ((0, 2),), -0.4, 0.0), -0.5, 0.5).astype(jnp.bfloat16),
        "g_ffn": jnp.clip(1.0 + 0.1 * jax.random.normal(keys[13], (N_SECTION, D), jnp.float32), 0.5, 1.5).astype(jnp.bfloat16),
        "b_ffn": jnp.clip(jax.random.uniform(keys[14], (N_SECTION, D), jnp.float32, -0.5, 0.5) * shard_levels(keys[14], (N_SECTION, D), ((0, 2),), -0.4, 0.0), -0.5, 0.5).astype(jnp.bfloat16),
    }


EPSILON = 1e-05
NEG_LARGE = -1e+30

@jax.custom_vjp
def low(v):
    return lax.optimization_barrier(v.astype(jnp.bfloat16)).astype(jnp.float32)

@jax.custom_vjp
def low_back(v):
    return v

def low_keep(v):
    return (low(v), None)

def low_pass(kept, grad):
    return (grad,)

def back_keep(v):
    return (v, None)

def back_low(kept, grad):
    return (low(grad),)
low.defvjp(low_keep, low_pass)
low_back.defvjp(back_keep, back_low)

def run_tables(seg_ids):
    length = seg_ids.shape[0]
    pad_id = SLOT // MINLEN
    same_run = seg_ids[:, None] == seg_ids[None, :]
    rows_at = lax.broadcasted_iota(jnp.int32, (length, length), 0)
    cols_at = lax.broadcasted_iota(jnp.int32, (length, length), 1)
    position = lax.optimization_barrier(jnp.sum(jnp.where(same_run & (cols_at < rows_at), 1.0, 0.0).astype(jnp.float32), axis=1))
    allowed = same_run & (seg_ids[None, :] < pad_id) | (rows_at == cols_at)
    halfway = HEAD // 2
    column = jnp.arange(halfway).astype(jnp.float32)
    frequency = jnp.exp(column * (-2.0 * math.log(10000.0) / HEAD))
    angles = position[:, None] * frequency[None, :]
    return (jnp.cos(angles)[:, None, :], jnp.sin(angles)[:, None, :], allowed)

def rotate(vector, cos_part, sin_part):
    halfway = vector.shape[-1] // 2
    first_half = vector[..., :halfway]
    second_half = vector[..., halfway:]
    return jnp.concatenate([first_half * cos_part - second_half * sin_part, second_half * cos_part + first_half * sin_part], axis=-1)

def layer_norm(values, gain_row, shift_row):
    centered = values - lax.optimization_barrier(jnp.mean(values, axis=-1, keepdims=True))
    spread = lax.optimization_barrier(jnp.mean(centered * centered, axis=-1, keepdims=True))
    return centered * lax.rsqrt(spread + EPSILON) * gain_row + shift_row

def encoder_layer(layer_input, cos_part, sin_part, allowed, weights):
    w_qkv, b_qkv, w_out, b_out, g_attn, b_attn, w_in, b_in, w_down, b_down, g_ffn, b_ffn = weights
    highest = lax.Precision.HIGHEST
    hidden = low_back(layer_input)
    length = hidden.shape[0]
    joined = low_back(jnp.dot(low(hidden), w_qkv, precision=highest) + b_qkv)
    split_heads = joined.reshape(length, 3, HEADS, HEAD)
    queries = low(rotate(split_heads[:, 0], cos_part, sin_part))
    keys_rot = low(rotate(split_heads[:, 1], cos_part, sin_part))
    values = low(split_heads[:, 2])
    scores = low_back(jnp.einsum('qhd,khd->hqk', queries, keys_rot, precision=highest) * (1.0 / math.sqrt(HEAD)))
    scores = jnp.where(allowed[None], scores, NEG_LARGE)
    probabilities = jax.nn.softmax(scores, axis=-1)
    attended = jnp.einsum('hqk,khd->qhd', low(probabilities), values, precision=highest).reshape(length, D)
    attended = low_back(low(attended))
    branch = low_back(jnp.dot(attended, w_out, precision=highest) + b_out)
    normed = layer_norm(hidden + branch, g_attn, b_attn)
    expanded = low_back(jnp.dot(low(normed), w_in, precision=highest) + b_in)
    activated = low(jax.nn.gelu(expanded, approximate=True))
    branch_two = low_back(jnp.dot(activated, w_down, precision=highest) + b_down)
    return low(layer_norm(normed + branch_two, g_ffn, b_ffn))

def reference(inputs, segments, cotangent, w_qkv, b_qkv, w_out, b_out, g_attn, b_attn, w_in, b_in, w_down, b_down, g_ffn, b_ffn):
    params = tuple((weight_arg.astype(jnp.float32) for weight_arg in (w_qkv, b_qkv, w_out, b_out, g_attn, b_attn, w_in, b_in, w_down, b_down, g_ffn, b_ffn)))
    run_count = MICRO * TOKENS // SLOT
    slot_inputs = inputs.reshape(run_count, SLOT, D).astype(jnp.float32)
    slot_cotangents = cotangent.reshape(run_count, SLOT, D).astype(jnp.float32)
    slot_segments = segments.reshape(run_count, SLOT)

    def one_run(totals, run_entry):
        run_input, run_cotangent, run_segments = run_entry
        cos_part, sin_part, allowed = run_tables(run_segments)
        real_rows = jnp.where(run_segments < SLOT // MINLEN, 1.0, 0.0).astype(jnp.float32)[:, None]

        def network(offsets, weights):
            hidden = run_input
            produced = []
            for section_id in range(N_SECTION):
                hidden = encoder_layer(hidden + offsets[section_id], cos_part, sin_part, allowed, [weight_arg[section_id] for weight_arg in weights])
                produced.append(hidden)
            return jnp.stack(produced)
        offsets = jnp.zeros((N_SECTION, SLOT, D), jnp.float32)
        produced, pullback = jax.vjp(network, offsets, params)
        seed_grad = jnp.zeros_like(produced).at[N_SECTION - 1].set(run_cotangent * real_rows)
        offset_grads, weight_grads = pullback(seed_grad)
        totals = tuple((running + extra_grad for running, extra_grad in zip(totals, weight_grads)))
        return (totals, (produced.astype(jnp.bfloat16), offset_grads.astype(jnp.bfloat16)))
    initial = tuple((jnp.zeros(weight_arg.shape, jnp.float32) for weight_arg in params))
    totals, (acts_runs, grad_runs) = lax.scan(one_run, initial, (slot_inputs, slot_cotangents, slot_segments))
    acts = jnp.transpose(acts_runs, (1, 0, 2, 3)).reshape(N_SECTION, MICRO, TOKENS, D)
    in_grads = jnp.transpose(grad_runs, (1, 0, 2, 3)).reshape(N_SECTION, MICRO, TOKENS, D)
    return (acts, in_grads, totals[0], totals[1], totals[2], totals[3], totals[4], totals[5], totals[6], totals[7], totals[8], totals[9], totals[10], totals[11])
```

```python
import functools
import math

import jax
import jax.numpy as jnp
from jax import lax
from jax.experimental import pallas as pl
from jax.experimental.pallas import tpu as pltpu
from jax.sharding import PartitionSpec as P

D = 768
HEADS = 12
HEAD = 64
PAIRS = HEADS // 2
SLOT = 512
MINLEN = 64
CHUNKS = 4
OUT = 2 * CHUNKS
QKV = OUT + 1
BLOCKS = QKV + 3
SEND_ORDER = (9, 10, 11, 8, 1, 0, 3, 2, 5, 4, 7, 6)
B_QKV, B_OUT, G_ATTN, B_ATTN, B_IN, B_DOWN, G_FFN, B_FFN = 0, 3, 4, 5, 6, 10, 11, 12
SMALL = 16
EPSILON = 1e-05
NEG_LARGE = -1e30
LOG2E = math.log2(math.e)
SCORE = LOG2E / math.sqrt(HEAD)
GELU_A = math.sqrt(2.0 / math.pi)
GELU_B = 0.044715
HALF = D // 2
MESH = pl.DeviceIdType.MESH
F32 = jnp.float32
BF16 = jnp.bfloat16
VMEM_LIMIT = 62 * 1024 * 1024


def dot(a, b):
    return lax.dot_general(a, b, (((1,), (0,)), ((), ())), preferred_element_type=F32)


def dot_t(a, b):
    return lax.dot_general(a, b, (((1,), (1,)), ((), ())), preferred_element_type=F32)


def swap_halves(t):
    lane = lax.broadcasted_iota(jnp.int32, t.shape, 1)
    return jnp.where(lane % HEAD < HEAD // 2, pltpu.roll(t, 96, 1), pltpu.roll(t, 32, 1))


def low_lanes(shape):
    return lax.broadcasted_iota(jnp.int32, shape, 1) < HEAD


def gelu_parts(u):
    square = u * u
    t = jnp.tanh(GELU_A * u * (1.0 + GELU_B * square))
    return square, t


def forward_kernel(
    inp, segr, segc, wq, wo, wi, wd, small,
    wall, xs, qkvs, lses, atts, n1s, nbs, us, n2s, rss, tabs, biases, acts, smalls,
    W, SM, X, QK, LSE, ATT, N1, NB, U, N2, RS, TAB, BIAS, ACC, ACT,
    osem, rsend, rrecv, ssem, wsem, stash, asem,
):
    sec = lax.axis_index("section")
    other = 1 - sec
    peer = {"section": other}
    tokens = X.shape[1]

    def source(b):
        if b < OUT:
            part = pl.ds(b // 2 * D, D)
            return wd.at[0, part, :] if b % 2 == 0 else wi.at[0, :, part]
        if b == OUT:
            return wo.at[0]
        return wq.at[0, :, pl.ds((b - QKV) * D, D)]

    def own_copy(b):
        return pltpu.make_async_copy(source(b), W.at[sec, b], osem.at[b])

    def peer_copy(b):
        return pltpu.make_async_remote_copy(
            source(b), W.at[sec, b], rsend.at[b], rrecv.at[b], device_id=peer, device_id_type=MESH
        )

    load_x = pltpu.make_async_copy(inp.at[sec], X.at[0], ssem.at[0])
    load_x.start()
    for b in SEND_ORDER[:4]:
        own_copy(b).start()
    barrier = pltpu.get_barrier_semaphore()
    pl.semaphore_signal(barrier, inc=1, device_id=peer, device_id_type=MESH)
    pl.semaphore_wait(barrier, 1)
    small_copy = pltpu.make_async_remote_copy(
        small, SM.at[sec], ssem.at[1], ssem.at[2], device_id=peer, device_id_type=MESH
    )
    small_copy.start()
    for b in SEND_ORDER:
        peer_copy(b).start()
    for b in SEND_ORDER[4:]:
        own_copy(b).start()
    SM[sec] = small[...]

    row_at = lax.broadcasted_iota(jnp.int32, (tokens, tokens), 0)
    col_at = lax.broadcasted_iota(jnp.int32, (tokens, tokens), 1)
    seg_col = segc[...]
    seg_row = segr[...]
    same = seg_col == seg_row
    position = jnp.sum(jnp.where(same & (col_at < row_at), 1.0, 0.0), axis=1, keepdims=True)
    allowed = (same & (seg_col < SLOT // MINLEN)) | (row_at == col_at)
    BIAS[...] = jnp.where(allowed, 0.0, NEG_LARGE)
    lane = lax.broadcasted_iota(jnp.int32, (1, 128), 1)
    frequency = jnp.exp((lane % 32).astype(F32) * (-2.0 * math.log(10000.0) / HEAD))
    angle = position * frequency
    TAB[0] = jnp.cos(angle)
    sine = jnp.sin(angle)
    TAB[1] = jnp.where(lane % HEAD < HEAD // 2, -sine, sine)
    table_out = pltpu.make_async_copy(TAB, tabs, ssem.at[3])
    table_out.start()
    bias_out = pltpu.make_async_copy(BIAS, biases, ssem.at[4])
    bias_out.start()
    load_x.wait()
    small_copy.wait()
    small_out = pltpu.make_async_copy(SM, smalls, ssem.at[5])
    small_out.start()

    def keep(k, layer, src, dst):
        pltpu.make_async_copy(src.at[layer], dst.at[layer], stash.at[layer, k]).start()

    def layer_step(layer, _):
        def ready(b):
            @pl.when(layer == sec)
            def _():
                pltpu.make_async_copy(wo.at[0], W.at[sec, b], osem.at[b]).wait()

            @pl.when(layer != sec)
            def _():
                pltpu.make_async_remote_copy(
                    wo.at[0], W.at[other, b], rsend.at[b], rrecv.at[b], device_id=peer, device_id_type=MESH
                ).wait_recv()

            pltpu.make_async_copy(W.at[layer, b], wall.at[layer, b], wsem.at[layer, b]).start()

        keep(0, layer, X, xs)
        for third in range(3):
            ready(QKV + third)

            def columns(c, _, third=third):
                cols = pl.ds(pl.multiple_of(c * 256, 256), 256)
                joined = dot(X[layer], W[layer, QKV + third, :, cols]) + SM[layer, B_QKV + third, :, cols]
                if third == 2:
                    QK[layer, third, :, cols] = joined.astype(BF16)
                else:
                    parts = []
                    for h in range(2):
                        t = joined[:, h * 128 : (h + 1) * 128]
                        parts.append((t * TAB[0] + swap_halves(t) * TAB[1]).astype(BF16))
                    QK[layer, third, :, cols] = jnp.concatenate(parts, axis=1)
                return 0

            lax.fori_loop(0, 3, columns, 0)
        keep(1, layer, QK, qkvs)

        def pair(hp, _):
            lanes = pl.ds(pl.multiple_of(hp * 128, 128), 128)
            q2 = QK[layer, 0, :, lanes]
            k2 = QK[layer, 1, :, lanes]
            v_t = QK[layer, 2, :, lanes].T
            low = low_lanes(k2.shape)
            outs = []
            for h in range(2):
                k_one = jnp.where(low if h == 0 else ~low, k2, jnp.zeros_like(k2))
                s = dot_t(k_one, q2) * SCORE + BIAS[...]
                peak = jnp.max(s, axis=0, keepdims=True)
                p = jnp.exp2(s - peak)
                total = jnp.sum(p, axis=0, keepdims=True)
                LSE[layer, hp, h : h + 1, :] = peak + jnp.log(total) * LOG2E
                outs.append(dot(v_t[h * HEAD : (h + 1) * HEAD], p.astype(BF16)) * (1.0 / total))
            ATT[layer, :, lanes] = jnp.concatenate(outs, axis=0).T.astype(BF16)
            return 0

        lax.fori_loop(0, PAIRS, pair, 0)
        keep(2, layer, LSE, lses)
        keep(3, layer, ATT, atts)
        ready(OUT)

        def norm_rows(r):
            mean = jnp.mean(r, axis=1, keepdims=True)
            centered = r - mean
            scale = lax.rsqrt(jnp.mean(centered * centered, axis=1, keepdims=True) + EPSILON)
            return centered * scale, scale

        def first_norm(c, _):
            rows = pl.ds(pl.multiple_of(c * 256, 256), 256)
            r = X[layer, rows, :].astype(F32) + dot(ATT[layer, rows, :], W[layer, OUT]) + SM[layer, B_OUT]
            n, scale = norm_rows(r)
            N1[layer, rows, :] = n.astype(BF16)
            RS[layer, 0, rows, :] = jnp.broadcast_to(scale, (256, 128))
            y = n * SM[layer, G_ATTN] + SM[layer, B_ATTN]
            NB[layer, rows, :] = y.astype(BF16)
            ACC[rows, :] = y + SM[layer, B_DOWN]
            return 0

        lax.fori_loop(0, tokens // 256, first_norm, 0)
        keep(4, layer, N1, n1s)
        keep(5, layer, NB, nbs)

        def ffn(f, _):
            ready(2 * f + 1)

            for c in range(3):
                cols = slice(c * 256, (c + 1) * 256)
                u = dot(NB[layer], W[layer, 2 * f + 1, :, cols]) + SM[layer, B_IN + f, :, cols]
                U[layer, f, :, cols] = u.astype(BF16)
                ACT[:, cols] = (0.5 * u * (1.0 + gelu_parts(u)[1])).astype(BF16)
            ready(2 * f)
            for c in range(3):
                cols = slice(c * 256, (c + 1) * 256)
                ACC[:, cols] += dot(ACT[...], W[layer, 2 * f, :, cols])
            return 0

        lax.fori_loop(0, CHUNKS, ffn, 0)
        keep(6, layer, U, us)

        def second_norm(c, _):
            rows = pl.ds(pl.multiple_of(c * 256, 256), 256)
            n, scale = norm_rows(ACC[rows, :])
            N2[layer, rows, :] = n.astype(BF16)
            RS[layer, 1, rows, :] = jnp.broadcast_to(scale, (256, 128))
            X[layer + 1, rows, :] = (n * SM[layer, G_FFN] + SM[layer, B_FFN]).astype(BF16)
            return 0

        lax.fori_loop(0, tokens // 256, second_norm, 0)
        keep(7, layer, N2, n2s)
        keep(8, layer, RS, rss)

        @pl.when(layer == sec)
        def _():
            pltpu.make_async_copy(X.at[layer + 1], acts.at[sec], asem.at[0]).start()

        @pl.when(layer != sec)
        def _():
            pltpu.make_async_remote_copy(
                X.at[layer + 1], acts.at[sec], asem.at[1], asem.at[2], device_id=peer, device_id_type=MESH
            ).start()

        return 0

    lax.fori_loop(0, 2, layer_step, 0)

    table_out.wait()
    bias_out.wait()
    small_out.wait()

    def finish(layer, _):
        for k, (src, dst) in enumerate(
            ((X, xs), (QK, qkvs), (LSE, lses), (ATT, atts), (N1, n1s), (NB, nbs), (U, us), (N2, n2s), (RS, rss))
        ):
            pltpu.make_async_copy(src.at[layer], dst.at[layer], stash.at[layer, k]).wait()
        for b in range(BLOCKS):
            pltpu.make_async_copy(W.at[layer, b], wall.at[layer, b], wsem.at[layer, b]).wait()
        return 0

    lax.fori_loop(0, 2, finish, 0)
    for b in range(BLOCKS):
        peer_copy(b).wait_send()
    pltpu.make_async_copy(X.at[1], acts.at[sec], asem.at[0]).wait()
    last = pltpu.make_async_remote_copy(
        X.at[1], acts.at[sec], asem.at[1], asem.at[2], device_id=peer, device_id_type=MESH
    )
    last.wait_send()
    last.wait_recv()


class Blocks:
    def __init__(self, G, RB, ST, peer_buf, outs, sems, dp, rep, dp_size, rep_size):
        self.G, self.RB, self.ST, self.peer_buf, self.outs = G, RB, ST, peer_buf, outs
        self.send, self.recv, self.load, self.out, self.peer_recv, self.peer_send, self.sync = sems
        self.dp, self.rep, self.n, self.rep_size = dp, rep, dp_size, rep_size
        self.line = dp_size == 4 and rep_size == 4
        self.ring = RB.shape[0]
        self.triples = 2 * BLOCKS // 3
        self.plans = {}
        self.steps = None
        for kind in (0, 1):
            self.steps = len(self.plan(jnp.int32(0), kind, jnp.int32(kind))) + 2
        assert self.steps - 1 < 2 * self.ring or self.ring >= self.triples

    def view(self, job, start, size):
        rows = pl.ds(pl.multiple_of(start, 16), size)
        cols = pl.ds(pl.multiple_of(job % 2 * HALF, 128), HALF)
        return self.G.at[job // 2, rows, cols]

    def landing(self, job, start, size):
        typ = job % 3
        return self.RB.at[job // 3 % self.ring, typ, pl.ds(pl.multiple_of(start, 16), size), :]

    def copy(self, job, k, src, dst, device):
        return pltpu.make_async_remote_copy(
            src, dst, self.send.at[job, k], self.recv.at[job, k], device_id=device, device_id_type=MESH
        )

    def add(self, job, start, place, size):
        step = 96 if size % 96 == 0 else 48
        g = self.view(job, start, size)
        r = self.landing(job, place, size)

        def body(i, _):
            rows = pl.ds(pl.multiple_of(i * step, 16), step)
            g[rows, :] = g[rows, :] + r[rows, :]
            return 0

        lax.fori_loop(0, size // step, body, 0)

    def move(self, job, start, place, size):
        g = self.view(job, start, size)
        r = self.landing(job, place, size)

        def body(i, _):
            rows = pl.ds(pl.multiple_of(i * 48, 16), 48)
            g[rows, :] = r[rows, :]
            return 0

        lax.fori_loop(0, size // 48, body, 0)

    def plan(self, job, kind, typ):
        self.sem_at = 0
        self.sync_at = 0
        self.place_at = 0
        if self.line:
            bits = [("rep", typ - 1), ("rep", 2 - typ)] if kind else [("rep", 0), ("rep", 1)]
            stages = bits + ["line"] if kind else ["line"] + bits
        else:
            stages = [("rep", b) for b in range(self.rep_size.bit_length() - 1)]
            stages += [("dp", b) for b in range(self.n.bit_length() - 1)]
        sizes, size = [], D
        for stage in stages:
            if stage == "line":
                size //= self.n
                sizes.append(size)
            elif self.halves(size):
                size //= 2
                sizes.append(size)
        start, size, cuts = jnp.int32(0), D, 0
        down, up = [], []
        for stage in stages:
            if stage == "line":
                cuts += 1
                start, size, a, b = self.line_stage(job, start, size, cuts == len(sizes))
            elif self.halves(size):
                cuts += 1
                start, size, a, b = self.pair_stage(job, start, size, *stage, cuts == len(sizes))
            else:
                a, b = self.swap_stage(job, start, size, *stage), []
            down = down + a
            up = b + up
        assert self.sem_at <= self.send.shape[1] and self.place_at <= self.RB.shape[2]
        assert self.sync_at <= self.sync.shape[1]
        return down + up

    @staticmethod
    def halves(size):
        return size // 2 % 48 == 0

    def take(self, sems, rows, syncs=0):
        k, place, y = self.sem_at, self.place_at, self.sync_at
        self.sem_at += sems
        self.place_at += rows
        self.sync_at += syncs
        return k, place, y

    def signal(self, job, y, device):
        pl.semaphore_signal(self.sync.at[job, y], inc=1, device_id=device, device_id_type=MESH)

    def swap_stage(self, job, start, size, axis, bit):
        index = self.rep if axis == "rep" else self.dp
        device = {axis: index ^ (1 << bit)}
        k, place, _ = self.take(1, size)

        def swap():
            return self.copy(job, k, self.view(job, start, size), self.landing(job, place, size), device)

        def finish():
            swap().wait()
            self.add(job, start, place, size)

        return [(lambda: swap().start(), finish, None, None)]

    def pair_stage(self, job, start, size, axis, bit, last):
        index = self.rep if axis == "rep" else self.dp
        mine = (index >> bit) & 1
        device = {axis: index ^ (1 << bit)}
        half = size // 2
        kept, given = start + mine * half, start + (1 - mine) * half
        k, place, y = self.take(2, 2 * half if last else half, 0 if last else 1)

        def down():
            return self.copy(job, k, self.view(job, given, half), self.landing(job, place, half), device)

        def up():
            there = self.landing(job, place + half, half) if last else self.view(job, kept, half)
            return self.copy(job, k + 1, self.view(job, kept, half), there, device)

        def finish_down():
            down().wait_recv()
            self.add(job, kept, place, half)

        def late():
            down().wait_send()
            if not last:
                self.signal(job, y, device)

        def start_up():
            if not last:
                pl.semaphore_wait(self.sync.at[job, y], 1)
            up().start()

        def finish_up():
            up().wait_recv()
            if last:
                down().wait_send()
                self.move(job, given, place + half, half)

        return (
            kept,
            half,
            [(lambda: down().start(), finish_down, None if last else late, None)],
            [(start_up, finish_up, None, lambda: up().wait_send())],
        )

    def line_stage(self, job, start, size, last):
        n, i = self.n, self.dp
        shard = size // n
        base, place, y = self.take(4 * (n - 1), (2 * n + 1 if last else n + 1) * shard, 0 if last else 2)
        right = {"dp": jnp.minimum(i + 1, n - 1)}
        left = {"dp": jnp.maximum(i - 1, 0)}

        def part(j):
            return self.view(job, start + j * shard, shard)

        def op(s, k, going_up):
            if going_up:
                send_r, send_l, take_r, take_l = i - s, i + s, i - 1 - s, i + 1 + s
                ok_sr, ok_sl = (i <= n - 2) & (send_r >= 0), (i >= 1) & (send_l <= n - 1)
                ok_tr, ok_tl = (i >= 1) & (take_r >= 0), (i <= n - 2) & (take_l <= n - 1)
            else:
                send_r, send_l, take_r, take_l = n - 1 - s + i, s + i - n + 1, n - 2 - s + i, s + i - n + 2
                ok_sr, ok_sl = (i <= n - 2) & (i <= s), (i >= 1) & (i >= n - 1 - s)
                ok_tr, ok_tl = (i >= 1) & (i - 1 <= s), (i <= n - 2) & (i >= n - 2 - s)

            def there(j, from_right):
                if going_up:
                    return self.landing(job, place + (n + 1 + j) * shard, shard) if last else part(j)
                slot = n if from_right and s == n - 2 else j
                return self.landing(job, place + slot * shard, shard)

            def to_right(j):
                return self.copy(job, k, part(j), there(j, False), right)

            def to_left(j):
                return self.copy(job, k + 1, part(j), there(j, True), left)

            def begin():
                if going_up and not last and s == 0:
                    pl.when(i >= 1)(lambda: pl.semaphore_wait(self.sync.at[job, y], 1))
                    pl.when(i <= n - 2)(lambda: pl.semaphore_wait(self.sync.at[job, y + 1], 1))
                pl.when(ok_sr)(lambda: to_right(send_r).start())
                pl.when(ok_sl)(lambda: to_left(send_l).start())

            def drain():
                pl.when(ok_sr)(lambda: to_right(send_r).wait_send())
                pl.when(ok_sl)(lambda: to_left(send_l).wait_send())

            def finish():
                def took(copy, j, slot):
                    copy.wait_recv()
                    if not going_up:
                        self.add(job, start + j * shard, place + slot * shard, shard)
                    elif last:
                        self.move(job, start + j * shard, place + (n + 1 + j) * shard, shard)

                if going_up and last and s == 0:
                    for one in down:
                        one[4]()
                pl.when(ok_tr)(lambda: took(to_right(take_r), take_r, take_r))
                pl.when(ok_tl)(lambda: took(to_left(take_l), take_l, n if s == n - 2 else take_l))

            def late():
                for one in down:
                    one[4]()
                pl.when(i <= n - 2)(lambda: self.signal(job, y, right))
                pl.when(i >= 1)(lambda: self.signal(job, y + 1, left))

            acked = not going_up and not last and s == n - 2
            return begin, finish, late if acked else None, drain if going_up else None, drain

        down = [op(s, base + 2 * s, False) for s in range(n - 1)]
        up = [op(s, base + 2 * (n - 1 + s), True) for s in range(n - 1)]
        return start + i * shard, shard, [one[:4] for one in down], [one[:4] for one in up]

    def peer_block(self, b):
        peer = {"section": 1 - lax.axis_index("section")}
        return pltpu.make_async_remote_copy(
            self.G.at[BLOCKS + b % 3],
            self.peer_buf.at[b],
            self.peer_send.at[b],
            self.peer_recv.at[b],
            device_id=peer,
            device_id_type=MESH,
        )

    def fetch(self, job):
        cols = pl.ds(pl.multiple_of(job % 2 * HALF, 128), HALF)
        return pltpu.make_async_copy(self.peer_buf.at[job // 2, :, cols], self.ST.at[job % 3], self.load.at[job % 3])

    def output(self, job):
        grad_q, grad_o, grad_i, grad_d = self.outs
        b, half = job // 2, pl.multiple_of(job % 2 * HALF, 128)
        src = self.G.at[b, :, pl.ds(half, HALF)]

        def to(dst):
            copy = pltpu.make_async_copy(src, dst, self.out.at[job])
            copy.start()

        pl.when((b < OUT) & (b % 2 == 0))(
            lambda: to(grad_d.at[pl.ds(pl.multiple_of(b // 2 % CHUNKS * D, D), D), pl.ds(half, HALF)])
        )
        pl.when((b < OUT) & (b % 2 == 1))(
            lambda: to(grad_i.at[:, pl.ds(pl.multiple_of(b // 2 % CHUNKS * D + half, 128), HALF)])
        )
        pl.when(b == OUT)(lambda: to(grad_o.at[:, pl.ds(half, HALF)]))
        pl.when(b > OUT)(
            lambda: to(grad_q.at[:, pl.ds(pl.multiple_of(jnp.maximum(b - QKV, 0) * D + half, 128), HALF)])
        )

    def step(self, triple, k, kind, typ):
        job = 3 * triple + typ
        if k == 0:

            @pl.when(job % 2 == 0)
            def _():
                self.peer_block(job // 2).wait_recv()

            self.fetch(job).start()
            return
        ops = self.plan(job, kind, typ)
        if k == 1:
            self.fetch(job).wait()
            g = self.view(job, 0, D)
            stage = self.ST.at[typ]

            def body(i, _):
                rows = pl.ds(pl.multiple_of(i * 96, 96), 96)
                g[rows, :] = g[rows, :] + stage[rows, :]
                return 0

            lax.fori_loop(0, D // 96, body, 0)
        else:
            ops[k - 2][1]()
        if k - 1 < len(ops):
            ops[k - 1][0]()
        if k >= 3 and ops[k - 3][2] is not None:
            ops[k - 3][2]()
        if k - 1 == len(ops):
            for op in ops:
                if op[3] is not None:
                    op[3]()
            self.output(job)

    def slot(self, t):
        for k in reversed(range(self.steps)):
            triple = (t - k) >> 1

            @pl.when((((t - k) & 1) == 0) & (t >= k) & (triple < self.triples))
            def _(k=k, triple=triple):
                self.step(triple, k, 0, jnp.int32(0))

                def rest(typ, _):
                    self.step(triple, k, 1, typ)
                    return 0

                lax.fori_loop(1, 3, rest, 0)

    @property
    def slots(self):
        return 2 * (self.triples - 1) + self.steps


CALLS = 9


def backward_kernel(
    dp_size, rep_size,
    cot, segc, wall, xs, qkvs, lses, atts, n1s, nbs, us, n2s, rss, tabs, biases, smalls,
    grad_q, grad_o, grad_i, grad_d, grad_small, ing, peer_buf,
    G, RB, ST, WR, UP, N2, NB, DB, DJ, N1, ATT, QK, U, TA, TN, DN, TAB, BIAS, RS, LSE, SM, SG, SB, SP,
    wsem, lsem, usem, send, recv, load, out, peer_send, peer_recv, gsem, ssend, srecv, sync,
):
    sec = lax.axis_index("section")
    dp = lax.axis_index("dp")
    rep = lax.axis_index("rep")
    peer = {"section": 1 - sec}
    tokens = UP.shape[0]
    sums = Blocks(
        G, RB, ST, peer_buf, (grad_q, grad_o, grad_i, grad_d),
        (send, recv, load, out, peer_recv, peer_send, sync), dp, rep, dp_size, rep_size,
    )

    def weight(seq):
        layer, b = 1 - seq // BLOCKS, seq % BLOCKS
        return pltpu.make_async_copy(wall.at[layer, b], WR.at[b % 4], wsem.at[b % 4])

    def u_copy(layer, f):
        return pltpu.make_async_copy(us.at[layer, f], U.at[f % 2], usem.at[f % 2])

    def loads(layer):
        return (
            pltpu.make_async_copy(n2s.at[layer], N2, lsem.at[0]),
            pltpu.make_async_copy(nbs.at[layer], NB, lsem.at[1]),
            pltpu.make_async_copy(n1s.at[layer], N1, lsem.at[2]),
            pltpu.make_async_copy(atts.at[layer], ATT, lsem.at[3]),
            pltpu.make_async_copy(qkvs.at[layer], QK, lsem.at[4]),
            pltpu.make_async_copy(rss.at[layer], RS, lsem.at[5]),
            pltpu.make_async_copy(lses.at[layer], LSE, lsem.at[6]),
            pltpu.make_async_copy(xs.at[layer], N2, lsem.at[7]),
        )

    first = (
        pltpu.make_async_copy(cot.at[sec], UP, lsem.at[8]),
        pltpu.make_async_copy(smalls, SM, lsem.at[9]),
        pltpu.make_async_copy(tabs, TAB, lsem.at[10]),
        pltpu.make_async_copy(biases, BIAS, lsem.at[11]),
    )
    for copy in first:
        copy.start()

    barrier = pltpu.get_barrier_semaphore()
    partners = [(peer, None)]
    partners += [({"rep": rep ^ (1 << b)}, None) for b in range(rep_size.bit_length() - 1)]
    partners += [({"dp": dp ^ (1 << b)}, None) for b in range(dp_size.bit_length() - 1)]
    if sums.line:
        partners += [({"dp": jnp.minimum(dp + 1, dp_size - 1)}, dp < dp_size - 1)]
        partners += [({"dp": jnp.maximum(dp - 1, 0)}, dp > 0)]
    count = 0
    for device, valid in partners:

        def greet(device=device):
            pl.semaphore_signal(barrier, inc=1, device_id=device, device_id_type=MESH)

        if valid is None:
            greet()
            count = count + 1
        else:
            pl.when(valid)(greet)
            count = count + jnp.where(valid, 1, 0)
    pl.semaphore_wait(barrier, count)

    for seq in range(4):
        weight(seq).start()
    real = jnp.where(segc[...] < SLOT // MINLEN, 1.0, 0.0).astype(F32)

    def in_copies(layer):
        mine = pltpu.make_async_copy(UP, ing.at[sec], gsem.at[0])
        theirs = pltpu.make_async_remote_copy(
            UP, ing.at[sec], gsem.at[1], gsem.at[2], device_id=peer, device_id_type=MESH
        )
        return mine, theirs

    def layer_step(li, _):
        layer = 1 - li
        copies = loads(layer)
        for copy in copies[:7]:
            copy.start()
        u_copy(layer, 0).start()
        u_copy(layer, 1).start()

        def target(b):
            return jnp.where(layer == sec, b, BLOCKS + b % 3)

        def slot(s):
            sums.slot((li - (1 - sec)) * CALLS + s)

        def before_block(b):
            @pl.when((layer != sec) & (b >= 3))
            def _():
                sums.peer_block(b - 3).wait_send()

        def after_block(b):
            @pl.when(layer != sec)
            def _():
                sums.peer_block(b).start()

        def outer(lhs_t, rhs, b):
            before_block(b)
            t = target(b)

            def columns(c, _):
                cols = pl.ds(pl.multiple_of(c * 256, 256), 256)
                G[t, :, cols] = dot(lhs_t[...], rhs[:, cols]).astype(BF16)
                return 0

            lax.fori_loop(0, 3, columns, 0)
            after_block(b)

        @pl.when(li == 0)
        def _():
            for copy in first:
                copy.wait()
            UP[...] = (UP[...].astype(F32) * real).astype(BF16)

        copies[0].wait()
        copies[5].wait()

        def norm_back(grad, n, gain, scale):
            a = grad * gain
            m1 = jnp.mean(a, axis=1, keepdims=True)
            m2 = jnp.mean(a * n, axis=1, keepdims=True)
            return (a - m1 - n * m2) * scale

        def rows_sum(value):
            return jnp.sum(value, axis=0, keepdims=True)

        for row in (G_FFN, B_FFN, B_DOWN, G_ATTN, B_ATTN, B_OUT):
            SG[layer, row] = jnp.zeros((1, D), F32)
        for row in (13, 14, 15):
            SG[layer, row] = jnp.zeros((1, D), F32)

        def second_norm(c, _):
            rows = pl.ds(pl.multiple_of(c * 256, 256), 256)
            up = UP[rows, :].astype(F32)
            n = N2[rows, :].astype(F32)
            scale = RS[1, rows, 0:1]
            g = norm_back(up, n, SM[layer, G_FFN], scale)
            DN[rows, :] = g
            DB[rows, :] = g.astype(BF16)
            SG[layer, G_FFN] += rows_sum(up * n)
            SG[layer, B_FFN] += rows_sum(up)
            SG[layer, B_DOWN] += rows_sum(g)
            return 0

        lax.fori_loop(0, tokens // 256, second_norm, 0)
        copies[7].start()
        copies[1].wait()
        TN[...] = NB[...].T

        def ffn(f, _):
            u_copy(layer, f).wait()
            weight(li * BLOCKS + 2 * f).wait()
            weight(li * BLOCKS + 2 * f + 1).wait()
            down, up = WR.at[2 * f % 4], WR.at[(2 * f + 1) % 4]
            for c in range(3):
                cols = slice(c * 256, (c + 1) * 256)
                u = U[f % 2, :, cols].astype(F32)
                square, t = gelu_parts(u)
                lift = 1.0 + t
                DJ[1, :, cols] = (0.5 * u * lift).astype(BF16)
                slope = 0.5 * lift * (1.0 + u * (1.0 - t) * (GELU_A * (1.0 + 3.0 * GELU_B * square)))
                grad = dot_t(DB[...], down[cols, :]) * slope
                SG[layer, B_IN + f, :, cols] = rows_sum(grad)
                DJ[0, :, cols] = grad.astype(BF16)
            TA[...] = DJ[1].T
            outer(TA, DB, 2 * f)
            outer(TN, DJ.at[0], 2 * f + 1)
            for c in range(3):
                cols = slice(c * 256, (c + 1) * 256)
                DN[:, cols] += dot_t(DJ[0], up[cols, :])
            weight(li * BLOCKS + 2 * f + 4).start()
            weight(li * BLOCKS + 2 * f + 5).start()
            pl.when(f + 2 < CHUNKS)(lambda: u_copy(layer, f + 2).start())
            slot(f)
            return 0

        lax.fori_loop(0, CHUNKS, ffn, 0)
        copies[2].wait()

        def first_norm(c, _):
            rows = pl.ds(pl.multiple_of(c * 256, 256), 256)
            up = DN[rows, :]
            n = N1[rows, :].astype(F32)
            g = norm_back(up, n, SM[layer, G_ATTN], RS[0, rows, 0:1])
            DN[rows, :] = g
            DB[rows, :] = g.astype(BF16)
            SG[layer, G_ATTN] += rows_sum(up * n)
            SG[layer, B_ATTN] += rows_sum(up)
            SG[layer, B_OUT] += rows_sum(g)
            return 0

        lax.fori_loop(0, tokens // 256, first_norm, 0)
        copies[3].wait()
        TA[...] = ATT[...].T
        outer(TA, DB, OUT)
        weight(li * BLOCKS + OUT).wait()
        w_out = WR.at[OUT % 4]
        for c in range(3):
            cols = slice(c * 256, (c + 1) * 256)
            NB[:, cols] = dot_t(DB[...], w_out[cols, :]).astype(BF16)
        pl.when(li == 0)(lambda: weight(BLOCKS).start())
        slot(CHUNKS)
        copies[4].wait()
        copies[6].wait()

        def pair(hp, _):
            lanes = pl.ds(pl.multiple_of(hp * 128, 128), 128)
            q2 = QK[0, :, lanes]
            k2 = QK[1, :, lanes]
            v2 = QK[2, :, lanes]
            o2 = NB[:, lanes]
            low = low_lanes(k2.shape)
            k_t = k2.T
            zero = jnp.zeros_like(k2)
            grads_q, grads_k, grads_v = [], [], []
            for h in range(2):
                mask = low if h == 0 else ~low
                s = dot_t(jnp.where(mask, k2, zero), q2) * SCORE + BIAS[...]
                p = jnp.exp2(s - LSE[hp, h : h + 1, :])
                dprob = dot_t(jnp.where(mask, v2, zero), o2)
                inner = jnp.sum(p * dprob, axis=0, keepdims=True)
                ds = (p * (dprob - inner)).astype(BF16)
                grads_v.append(dot(p.astype(BF16), o2))
                grads_k.append(dot(ds, q2))
                grads_q.append(dot(k_t[h * HEAD : (h + 1) * HEAD], ds))
            scale = 1.0 / math.sqrt(HEAD)
            gq = jnp.concatenate(grads_q, axis=0).T * scale
            gk = jnp.where(low, grads_k[0], grads_k[1]) * scale
            gv = jnp.where(low, grads_v[0], grads_v[1])
            cos, sin = TAB[0], TAB[1]
            gq = gq * cos - swap_halves(gq) * sin
            gk = gk * cos - swap_halves(gk) * sin
            for third, g in enumerate((gq, gk, gv)):
                DJ[third, :, lanes] = g.astype(BF16)
                SG[layer, B_QKV + third, :, lanes] = rows_sum(g)
            pl.when(hp % 2 == 1)(lambda: slot(CHUNKS + 1 + hp // 2))
            return 0

        lax.fori_loop(0, PAIRS, pair, 0)
        copies[7].wait()
        TN[...] = N2[...].T

        def third_step(third, _):
            outer(TN, DJ.at[third], QKV + third)
            weight(li * BLOCKS + QKV + third).wait()
            w = WR.at[(QKV + third) % 4]
            for c in range(3):
                cols = slice(c * 256, (c + 1) * 256)
                DN[:, cols] += dot_t(DJ[third], w[cols, :])
            pl.when(li == 0)(lambda: weight(BLOCKS + 1 + third).start())
            return 0

        lax.fori_loop(0, 3, third_step, 0)

        @pl.when(layer != sec)
        def _():
            for b in range(BLOCKS - 3, BLOCKS):
                sums.peer_block(b).wait_send()

        mine, theirs = in_copies(layer)
        @pl.when(li == 1)
        def _():
            pl.when(sec == 1)(lambda: mine.wait())
            pl.when(sec == 0)(lambda: theirs.wait_send())

        UP[...] = DN[...].astype(BF16)
        pl.when(layer == sec)(lambda: mine.start())
        pl.when(layer != sec)(lambda: theirs.start())
        slot(CALLS - 1)
        return 0

    lax.fori_loop(0, 2, layer_step, 0)

    small_partners = [peer] + [device for device, valid in partners[1:] if valid is None]

    def small_copy(m):
        src = SG.at[1 - sec] if m == 0 else SP.at[m - 1]
        return pltpu.make_async_remote_copy(
            src, SB.at[m], ssend.at[m], srecv.at[m], device_id=small_partners[m], device_id_type=MESH
        )

    small_copy(0).start()

    def small_step(m):
        small_copy(m).wait_recv()
        SP[m] = (SG[sec] if m == 0 else SP[m - 1]) + SB[m]
        if m + 1 < len(small_partners):
            small_copy(m + 1).start()

    rounds = max(sums.slots - CALLS, len(small_partners))

    def final(i, _):
        sums.slot((1 + sec) * CALLS + i)
        for m in range(len(small_partners)):
            pl.when(i == m)(functools.partial(small_step, m))
        return 0

    lax.fori_loop(0, rounds, final, 0)
    for m in range(len(small_partners)):
        small_copy(m).wait_send()
    small_out = pltpu.make_async_copy(SP.at[len(small_partners) - 1], grad_small, ssend.at[0])
    small_out.start()

    def out_wait(job, _):
        pltpu.make_async_copy(G.at[0, :, pl.ds(0, HALF)], grad_o.at[:, pl.ds(0, HALF)], out.at[job]).wait()
        return 0

    lax.fori_loop(0, 2 * BLOCKS, out_wait, 0)
    small_out.wait()
    mine, theirs = in_copies(0)
    pl.when(sec == 0)(lambda: mine.wait())
    pl.when(sec == 1)(lambda: theirs.wait_send())
    theirs.wait_recv()


def per_device(
    dp_size, rep_size, inputs, segments, cotangent, w_qkv, b_qkv, w_out, b_out, g_attn, b_attn, w_in, b_in, w_down,
    b_down, g_ffn, b_ffn,
):
    sec = lax.axis_index("section")
    tokens = inputs.shape[1]
    own = lax.dynamic_index_in_dim(segments, sec, 0, keepdims=False)
    rows = [b_qkv.reshape(3, D), b_out, g_attn, b_attn, b_in.reshape(CHUNKS, D), b_down, g_ffn, b_ffn]
    small = jnp.concatenate([row.astype(F32) for row in rows] + [jnp.zeros((3, D), F32)], axis=0)
    small = small.reshape(SMALL, 1, D)
    anywhere = pl.BlockSpec(memory_space=pl.ANY)
    in_vmem = pl.BlockSpec(memory_space=pltpu.VMEM)

    def shape(*dims, dtype=BF16):
        return jax.ShapeDtypeStruct(dims, dtype)

    def mem(*dims, dtype=BF16):
        return pltpu.VMEM(dims, dtype)

    dma = pltpu.SemaphoreType.DMA
    stash = pl.pallas_call(
        forward_kernel,
        out_shape=(
            shape(2, BLOCKS, D, D),
            shape(2, tokens, D),
            shape(2, 3, tokens, D),
            shape(2, PAIRS, 8, tokens, dtype=F32),
            shape(2, tokens, D),
            shape(2, tokens, D),
            shape(2, tokens, D),
            shape(2, CHUNKS, tokens, D),
            shape(2, tokens, D),
            shape(2, 2, tokens, 128, dtype=F32),
            shape(2, tokens, 128, dtype=F32),
            shape(tokens, tokens, dtype=F32),
            shape(2, tokens, D),
            shape(2, SMALL, 1, D, dtype=F32),
        ),
        in_specs=[anywhere, in_vmem, in_vmem] + [anywhere] * 4 + [in_vmem],
        out_specs=(anywhere,) * 14,
        scratch_shapes=[
            mem(2, BLOCKS, D, D),
            mem(2, SMALL, 1, D, dtype=F32),
            mem(3, tokens, D),
            mem(2, 3, tokens, D),
            mem(2, PAIRS, 8, tokens, dtype=F32),
            mem(2, tokens, D),
            mem(2, tokens, D),
            mem(2, tokens, D),
            mem(2, CHUNKS, tokens, D),
            mem(2, tokens, D),
            mem(2, 2, tokens, 128, dtype=F32),
            mem(2, tokens, 128, dtype=F32),
            mem(tokens, tokens, dtype=F32),
            mem(tokens, D, dtype=F32),
            mem(tokens, D),
            dma((BLOCKS,)),
            dma((BLOCKS,)),
            dma((BLOCKS,)),
            dma((6,)),
            dma((2, BLOCKS)),
            dma((2, 9)),
            dma((3,)),
        ],
        compiler_params=pltpu.CompilerParams(collective_id=0, has_side_effects=True, vmem_limit_bytes=VMEM_LIMIT),
        name="forward",
    )(inputs, own.reshape(1, tokens), own.reshape(tokens, 1), w_qkv, w_out, w_in, w_down, small)
    (wall, xs, qkvs, lses, atts, n1s, nbs, us, n2s, rss, tabs, biases, acts, smalls) = stash

    line = dp_size == 4 and rep_size == 4
    bits = dp_size.bit_length() + rep_size.bit_length() - 2
    ring = 6 if line else 8
    landing = 1152 if line else 912
    sems = 16
    out = pl.pallas_call(
        functools.partial(backward_kernel, dp_size, rep_size),
        out_shape=(
            shape(D, 3 * D),
            shape(D, D),
            shape(D, CHUNKS * D),
            shape(CHUNKS * D, D),
            shape(SMALL, 1, D, dtype=F32),
            shape(2, tokens, D),
            shape(BLOCKS, D, D),
        ),
        in_specs=[anywhere, in_vmem] + [anywhere] * 13,
        out_specs=(anywhere,) * 7,
        scratch_shapes=[
            mem(BLOCKS + 3, D, D),
            mem(ring, 3, landing, HALF),
            mem(3, D, HALF),
            mem(4, D, D),
            mem(tokens, D),
            mem(tokens, D),
            mem(tokens, D),
            mem(tokens, D),
            mem(3, tokens, D),
            mem(tokens, D),
            mem(tokens, D),
            mem(3, tokens, D),
            mem(2, tokens, D),
            mem(D, tokens),
            mem(D, tokens),
            mem(tokens, D, dtype=F32),
            mem(2, tokens, 128, dtype=F32),
            mem(tokens, tokens, dtype=F32),
            mem(2, tokens, 128, dtype=F32),
            mem(PAIRS, 8, tokens, dtype=F32),
            mem(2, SMALL, 1, D, dtype=F32),
            mem(2, SMALL, 1, D, dtype=F32),
            mem(bits + 1, SMALL, 1, D, dtype=F32),
            mem(bits + 1, SMALL, 1, D, dtype=F32),
            dma((4,)),
            dma((12,)),
            dma((2,)),
            dma((2 * BLOCKS, sems)),
            dma((2 * BLOCKS, sems)),
            dma((3,)),
            dma((2 * BLOCKS,)),
            dma((BLOCKS,)),
            dma((BLOCKS,)),
            dma((3,)),
            dma((bits + 1,)),
            dma((bits + 1,)),
            pltpu.SemaphoreType.REGULAR((2 * BLOCKS, 4)),
        ],
        compiler_params=pltpu.CompilerParams(collective_id=1, has_side_effects=True, vmem_limit_bytes=VMEM_LIMIT),
        name="backward",
    )(cotangent, own.reshape(tokens, 1), wall, xs, qkvs, lses, atts, n1s, nbs, us, n2s, rss, tabs, biases, smalls)
    grad_q, grad_o, grad_i, grad_d, grad_small, ing, _ = out
    grads = grad_small.reshape(SMALL, D)

    def row(start, count=1):
        return grads[start : start + count].reshape(1, count * D)

    return (
        acts[None],
        ing[None],
        grad_q.astype(F32)[None],
        row(B_QKV, 3),
        grad_o.astype(F32)[None],
        row(B_OUT),
        row(G_ATTN),
        row(B_ATTN),
        grad_i.astype(F32)[None],
        row(B_IN, CHUNKS),
        grad_d.astype(F32)[None],
        row(B_DOWN),
        row(G_FFN),
        row(B_FFN),
    )


def solution(mesh):
    tokens = ("dp", "rep")
    weight, vector = P("section", None, None), P("section", None)
    weights = (weight, vector, weight, vector, vector, vector, weight, vector, weight, vector, vector, vector)
    activations = P("section", None, tokens, None)
    return jax.shard_map(
        functools.partial(per_device, mesh.shape["dp"], mesh.shape["rep"]),
        mesh=mesh,
        in_specs=(P(None, tokens, None), P(None, tokens), P(None, tokens, None), *weights),
        out_specs=(activations, activations, *weights),
        check_vma=False,
    )
```

```python
import functools
import math

import jax
import jax.numpy as jnp
from jax import lax
from jax.experimental import pallas as pl
from jax.experimental.pallas import tpu as pltpu
from jax.sharding import PartitionSpec as P

D = 768
HEADS = 12
HEAD = 64
PAIRS = HEADS // 2
SLOT = 512
MINLEN = 64
CHUNKS = 4
OUT = 2 * CHUNKS
QKV = OUT + 1
BLOCKS = QKV + 3
SEND_ORDER = (9, 10, 11, 8, 1, 0, 3, 2, 5, 4, 7, 6)
B_QKV, B_OUT, G_ATTN, B_ATTN, B_IN, B_DOWN, G_FFN, B_FFN = 0, 3, 4, 5, 6, 10, 11, 12
SMALL = 16
EPSILON = 1e-05
NEG_LARGE = -1e30
LOG2E = math.log2(math.e)
SCORE = LOG2E / math.sqrt(HEAD)
GELU_A = math.sqrt(2.0 / math.pi)
GELU_B = 0.044715
THIRD = D // 3
OWN = BLOCKS // 2
CALLS = 18
FINAL = 2 * CALLS
TABLE = (
    (1, 2, 5, 8, 11, 14, 17, 20, 23, 26, 29, 32),
    (3, 4, 7, 10, 13, 16, 19, 22, 25, 28, 31, 34),
    (5, 6, 9, 12, 15, 18, 21, 24, 27, 30, 33, 36),
    (7, 8, 11, 14, 17, 20, 23, 26, 29, 32, 35, 37),
    (15, 16, 19, 22, 25, 28, 31, 34, 36, 37, 38, 39),
    (17, 18, 21, 24, 27, 30, 33, 36, 37, 38, 39, 40),
    (19, 20, 23, 26, 29, 32, 35, 37, 38, 39, 40, 41),
    (21, 22, 25, 28, 31, 34, 36, 38, 39, 40, 41, 42),
    (23, 24, 27, 30, 33, 36, 37, 39, 40, 41, 42, 43),
    (25, 26, 29, 32, 35, 37, 38, 40, 41, 42, 43, 44),
    (33, 34, 36, 37, 38, 39, 40, 41, 42, 43, 44, 45),
    (35, 36, 37, 38, 39, 40, 41, 42, 43, 44, 45, 46),
)


def timetable(steps):
    ready = [CALLS * li + at for li in range(2) for at in (1, 3, 5, 7, 15, 17)]
    table = []
    for o, first in enumerate(ready):
        times = []
        for k in range(steps):
            t = max(first, times[-1] + 1 if k else 0, table[-1][k] + 1 if o else 0)
            times.append(t)
        table.append(times)
    return table


MESH = pl.DeviceIdType.MESH
F32 = jnp.float32
BF16 = jnp.bfloat16
VMEM_LIMIT = 62 * 1024 * 1024


def dot(a, b):
    return lax.dot_general(a, b, (((1,), (0,)), ((), ())), preferred_element_type=F32)


def dot_t(a, b):
    return lax.dot_general(a, b, (((1,), (1,)), ((), ())), preferred_element_type=F32)


def dot_tn(a, b):
    return lax.dot_general(a, b, (((0,), (0,)), ((), ())), preferred_element_type=F32)


def swap_halves(t):
    lane = lax.broadcasted_iota(jnp.int32, t.shape, 1)
    return jnp.where(lane % HEAD < HEAD // 2, pltpu.roll(t, 96, 1), pltpu.roll(t, 32, 1))


def low_lanes(shape):
    return lax.broadcasted_iota(jnp.int32, shape, 1) < HEAD


def own_segments(segs, sec):
    row = jnp.where(sec == 0, segs[0:1, :], segs[1:2, :]).astype(F32)
    return row, jnp.broadcast_to(row, (128, row.shape[1])).T[:, 0:1]


def gelu_parts(u):
    square = u * u
    t = jnp.tanh(GELU_A * u * (1.0 + GELU_B * square))
    return square, t


def forward_kernel(
    inp, segs, wq, wo, wi, wd, bq, bo, ga, ba, bi, bd, gf, bf,
    wall, xs, qkvs, lses, atts, n1s, nbs, us, n2s, rss, tabs, biases, acts, smalls,
    W, SM, X, QK, LSE, ATT, N1, NB, U, N2, RS, TAB, BIAS, ACC, ACT,
    osem, rsend, rrecv, ssem, wsem, stash, asem,
):
    sec = lax.axis_index("section")
    other = 1 - sec
    peer = {"section": other}
    tokens = X.shape[1]

    def source(b):
        if b < OUT:
            part = pl.ds(b // 2 * D, D)
            return wd.at[0, part, :] if b % 2 == 0 else wi.at[0, :, part]
        if b == OUT:
            return wo.at[0]
        return wq.at[0, :, pl.ds((b - QKV) * D, D)]

    def own_copy(b):
        return pltpu.make_async_copy(source(b), W.at[sec, b], osem.at[b])

    def peer_copy(b):
        return pltpu.make_async_remote_copy(
            source(b), W.at[sec, b], rsend.at[b], rrecv.at[b], device_id=peer, device_id_type=MESH
        )

    load_x = pltpu.make_async_copy(inp.at[sec], X.at[0], ssem.at[0])
    load_x.start()
    for b in SEND_ORDER[:4]:
        own_copy(b).start()
    barrier = pltpu.get_barrier_semaphore()
    pl.semaphore_signal(barrier, inc=1, device_id=peer, device_id_type=MESH)
    pl.semaphore_wait(barrier, 1)
    for row, ref in ((B_QKV, bq), (B_OUT, bo), (G_ATTN, ga), (B_ATTN, ba), (B_IN, bi), (B_DOWN, bd), (G_FFN, gf), (B_FFN, bf)):
        for i in range(ref.shape[1] // D):
            SM[sec, row + i] = ref[0:1, i * D : (i + 1) * D].astype(F32)
    for row in range(B_FFN + 1, SMALL):
        SM[sec, row] = jnp.zeros((1, D), F32)
    small_copy = pltpu.make_async_remote_copy(
        SM.at[sec], SM.at[sec], ssem.at[1], ssem.at[2], device_id=peer, device_id_type=MESH
    )
    small_copy.start()
    for b in SEND_ORDER:
        peer_copy(b).start()
    for b in SEND_ORDER[4:]:
        own_copy(b).start()

    row_at = lax.broadcasted_iota(jnp.int32, (tokens, tokens), 0)
    col_at = lax.broadcasted_iota(jnp.int32, (tokens, tokens), 1)
    seg_row, seg_col = own_segments(segs, sec)
    same = seg_col == seg_row
    position = jnp.sum(jnp.where(same & (col_at < row_at), 1.0, 0.0), axis=1, keepdims=True)
    allowed = (same & (seg_col < SLOT // MINLEN)) | (row_at == col_at)
    BIAS[...] = jnp.where(allowed, 0.0, NEG_LARGE)
    lane = lax.broadcasted_iota(jnp.int32, (1, 128), 1)
    frequency = jnp.exp((lane % 32).astype(F32) * (-2.0 * math.log(10000.0) / HEAD))
    angle = position * frequency
    TAB[0] = jnp.cos(angle)
    sine = jnp.sin(angle)
    TAB[1] = jnp.where(lane % HEAD < HEAD // 2, -sine, sine)
    table_out = pltpu.make_async_copy(TAB, tabs, ssem.at[3])
    table_out.start()
    bias_out = pltpu.make_async_copy(BIAS, biases, ssem.at[4])
    bias_out.start()
    load_x.wait()
    small_copy.wait()
    small_out = pltpu.make_async_copy(SM, smalls, ssem.at[5])
    small_out.start()

    def keep(k, layer, src, dst):
        pltpu.make_async_copy(src.at[layer], dst.at[layer], stash.at[layer, k]).start()

    def layer_step(layer, _):
        def ready(b):
            @pl.when(layer == sec)
            def _():
                pltpu.make_async_copy(wo.at[0], W.at[sec, b], osem.at[b]).wait()

            @pl.when(layer != sec)
            def _():
                pltpu.make_async_remote_copy(
                    wo.at[0], W.at[other, b], rsend.at[b], rrecv.at[b], device_id=peer, device_id_type=MESH
                ).wait_recv()

            pltpu.make_async_copy(W.at[layer, b], wall.at[layer, b], wsem.at[layer, b]).start()

        keep(0, layer, X, xs)
        for third in range(3):
            ready(QKV + third)

            for c in range(3):
                cols = slice(c * 256, (c + 1) * 256)
                joined = dot(X[layer], W[layer, QKV + third, :, cols]) + SM[layer, B_QKV + third, :, cols]
                if third == 2:
                    QK[layer, third, :, cols] = joined.astype(BF16)
                else:
                    parts = []
                    for h in range(2):
                        t = joined[:, h * 128 : (h + 1) * 128]
                        parts.append((t * TAB[0] + swap_halves(t) * TAB[1]).astype(BF16))
                    QK[layer, third, :, cols] = jnp.concatenate(parts, axis=1)
        keep(1, layer, QK, qkvs)

        def pair(hp, _):
            lanes = pl.ds(pl.multiple_of(hp * 128, 128), 128)
            q2 = QK[layer, 0, :, lanes]
            k2 = QK[layer, 1, :, lanes]
            v_t = QK[layer, 2, :, lanes].T
            low = low_lanes(k2.shape)
            outs = []
            for h in range(2):
                k_one = jnp.where(low if h == 0 else ~low, k2, jnp.zeros_like(k2))
                s = dot_t(k_one, q2) * SCORE + BIAS[...]
                peak = jnp.max(s, axis=0, keepdims=True)
                p = jnp.exp2(s - peak)
                total = jnp.sum(p, axis=0, keepdims=True)
                LSE[layer, hp, h : h + 1, :] = peak + jnp.log(total) * LOG2E
                outs.append(dot(v_t[h * HEAD : (h + 1) * HEAD], p.astype(BF16)) * (1.0 / total))
            ATT[layer, :, lanes] = jnp.concatenate(outs, axis=0).T.astype(BF16)
            return 0

        lax.fori_loop(0, PAIRS, pair, 0)
        keep(2, layer, LSE, lses)
        keep(3, layer, ATT, atts)
        ready(OUT)

        def norm_rows(r):
            mean = jnp.mean(r, axis=1, keepdims=True)
            centered = r - mean
            scale = lax.rsqrt(jnp.mean(centered * centered, axis=1, keepdims=True) + EPSILON)
            return centered * scale, scale

        def first_norm(c, _):
            rows = pl.ds(pl.multiple_of(c * 256, 256), 256)
            r = X[layer, rows, :].astype(F32) + dot(ATT[layer, rows, :], W[layer, OUT]) + SM[layer, B_OUT]
            n, scale = norm_rows(r)
            N1[layer, rows, :] = n.astype(BF16)
            RS[layer, 0, rows, :] = jnp.broadcast_to(scale, (256, 128))
            y = n * SM[layer, G_ATTN] + SM[layer, B_ATTN]
            NB[layer, rows, :] = y.astype(BF16)
            ACC[rows, :] = y + SM[layer, B_DOWN]
            return 0

        lax.fori_loop(0, tokens // 256, first_norm, 0)
        keep(4, layer, N1, n1s)
        keep(5, layer, NB, nbs)

        def ffn(f, _):
            ready(2 * f + 1)

            for c in range(3):
                cols = slice(c * 256, (c + 1) * 256)
                u = dot(NB[layer], W[layer, 2 * f + 1, :, cols]) + SM[layer, B_IN + f, :, cols]
                U[layer, f, :, cols] = u.astype(BF16)
                ACT[:, cols] = (0.5 * u * (1.0 + gelu_parts(u)[1])).astype(BF16)
            ready(2 * f)
            for c in range(3):
                cols = slice(c * 256, (c + 1) * 256)
                ACC[:, cols] += dot(ACT[...], W[layer, 2 * f, :, cols])
            return 0

        lax.fori_loop(0, CHUNKS, ffn, 0)
        keep(6, layer, U, us)

        def second_norm(c, _):
            rows = pl.ds(pl.multiple_of(c * 256, 256), 256)
            n, scale = norm_rows(ACC[rows, :])
            N2[layer, rows, :] = n.astype(BF16)
            RS[layer, 1, rows, :] = jnp.broadcast_to(scale, (256, 128))
            X[layer + 1, rows, :] = (n * SM[layer, G_FFN] + SM[layer, B_FFN]).astype(BF16)
            return 0

        lax.fori_loop(0, tokens // 256, second_norm, 0)
        keep(7, layer, N2, n2s)
        keep(8, layer, RS, rss)

        @pl.when(layer == sec)
        def _():
            pltpu.make_async_copy(X.at[layer + 1], acts.at[sec], asem.at[0]).start()

        @pl.when(layer != sec)
        def _():
            pltpu.make_async_remote_copy(
                X.at[layer + 1], acts.at[sec], asem.at[1], asem.at[2], device_id=peer, device_id_type=MESH
            ).start()

        return 0

    lax.fori_loop(0, 2, layer_step, 0)

    table_out.wait()
    bias_out.wait()
    small_out.wait()

    def finish(layer, _):
        for k, (src, dst) in enumerate(
            ((X, xs), (QK, qkvs), (LSE, lses), (ATT, atts), (N1, n1s), (NB, nbs), (U, us), (N2, n2s), (RS, rss))
        ):
            pltpu.make_async_copy(src.at[layer], dst.at[layer], stash.at[layer, k]).wait()
        for b in range(BLOCKS):
            pltpu.make_async_copy(W.at[layer, b], wall.at[layer, b], wsem.at[layer, b]).wait()
        return 0

    lax.fori_loop(0, 2, finish, 0)
    for b in range(BLOCKS):
        peer_copy(b).wait_send()
    pltpu.make_async_copy(X.at[1], acts.at[sec], asem.at[0]).wait()
    last = pltpu.make_async_remote_copy(
        X.at[1], acts.at[sec], asem.at[1], asem.at[2], device_id=peer, device_id_type=MESH
    )
    last.wait_send()
    last.wait_recv()


class Blocks:
    def __init__(self, G, RB, ST, peer_buf, outs, sems, dp, rep, dp_size, rep_size):
        self.G, self.RB, self.ST, self.peer_buf, self.outs = G, RB, ST, peer_buf, outs
        (self.send, self.recv, self.load, self.out, self.out_recv, self.peer_recv, self.peer_send, self.sync) = sems
        self.sec, self.dp, self.rep, self.n, self.rep_size = lax.axis_index("section"), dp, rep, dp_size, rep_size
        self.line = dp_size == 4 and rep_size == 4
        self.ring = RB.shape[0]
        for kind in (0, 1):
            self.steps = len(self.plan(jnp.int32(0), kind, jnp.int32(kind))) + 2
        self.table = TABLE if self.steps == len(TABLE[0]) else timetable(self.steps)

    def view(self, job, start, size):
        block, typ = job
        rows = pl.ds(pl.multiple_of(start, 16), size)
        cols = pl.ds(pl.multiple_of(typ * THIRD, 128), THIRD)
        return self.G.at[block, rows, cols]

    def landing(self, job, start, size):
        block, typ = job
        return self.RB.at[block % self.ring, typ, pl.ds(pl.multiple_of(start, 16), size), :]

    def copy(self, job, k, src, dst, device, side=0):
        block, typ = job
        slot = block % self.ring * 3 + typ
        return pltpu.make_async_remote_copy(
            src, dst, self.send.at[slot, side], self.recv.at[slot, k], device_id=device, device_id_type=MESH
        )

    def combine(self, job, start, place, size, add):
        step = 96 if size % 96 == 0 else 48
        g = self.view(job, start, size)
        r = self.landing(job, place, size)

        def body(i, _):
            rows = pl.ds(pl.multiple_of(i * step, 16), step)
            g[rows, :] = g[rows, :] + r[rows, :] if add else r[rows, :]
            return 0

        lax.fori_loop(0, size // step, body, 0)

    def plan(self, job, kind, typ):
        if not isinstance(job, tuple):
            job = (job, typ)
        self.sem_at = 0
        self.sync_at = 0
        self.place_at = 0
        if self.line:
            bits = [("rep", typ - 1), ("rep", 2 - typ)] if kind else [("rep", job[0] & 1), ("rep", 1 - (job[0] & 1))]
            stages = bits + ["line"] if kind else ["line"] + bits
        else:
            stages = [("rep", b) for b in range(self.rep_size.bit_length() - 1)]
            stages += [("dp", b) for b in range(self.n.bit_length() - 1)]
        total, size = 0, D
        for stage in stages:
            if stage == "line":
                size //= self.n
                total += 1
            elif self.halves(size):
                size //= 2
                total += 1
        start, size, cuts = jnp.int32(0), D, 0
        down, up = [], []
        for stage in stages:
            if stage == "line":
                cuts += 1
                start, size, a, b = self.line_stage(job, start, size, cuts == total)
            elif self.halves(size):
                cuts += 1
                start, size, a, b = self.pair_stage(job, start, size, *stage, cuts == total)
            else:
                a, b = self.swap_stage(job, start, size, *stage), []
            down = down + a
            up = b + up
        assert self.sem_at <= self.recv.shape[1] and self.place_at <= self.RB.shape[2]
        assert self.sync_at <= self.sync.shape[1]
        return down + up

    @staticmethod
    def halves(size):
        return size // 2 % 48 == 0

    def take(self, sems, rows, syncs=0):
        k, place, y = self.sem_at, self.place_at, self.sync_at
        self.sem_at += sems
        self.place_at += rows
        self.sync_at += syncs
        return k, place, y

    def ack(self, job, y):
        return self.sync.at[job[0] % self.ring * 3 + job[1], y]

    def signal(self, job, y, device):
        pl.semaphore_signal(self.ack(job, y), inc=1, device_id=device, device_id_type=MESH)

    def swap_stage(self, job, start, size, axis, bit):
        index = self.rep if axis == "rep" else self.dp
        device = {axis: index ^ (1 << bit)}
        k, place, _ = self.take(1, size)

        def swap():
            return self.copy(job, k, self.view(job, start, size), self.landing(job, place, size), device)

        def finish():
            swap().wait()
            self.combine(job, start, place, size, True)

        return [(lambda: swap().start(), finish)]

    def pair_stage(self, job, start, size, axis, bit, last):
        index = self.rep if axis == "rep" else self.dp
        mine = (index >> bit) & 1
        device = {axis: index ^ (1 << bit)}
        half = size // 2
        kept, given = start + mine * half, start + (1 - mine) * half
        k, place, y = self.take(2 if last else 1, 2 * half if last else half, 0 if last else 1)

        def down():
            return self.copy(job, k, self.view(job, given, half), self.landing(job, place, half), device)

        def up():
            there = self.landing(job, place + half, half) if last else self.view(job, kept, half)
            return self.copy(job, k + 1 if last else k, self.view(job, kept, half), there, device)

        def finish_down():
            down().wait_recv()
            self.combine(job, kept, place, half, True)
            down().wait_send()
            if not last:
                self.signal(job, y, device)

        def start_up():
            if not last:
                pl.semaphore_wait(self.ack(job, y), 1)
            up().start()

        def finish_up():
            up().wait()
            if last:
                self.combine(job, given, place + half, half, False)

        return kept, half, [(lambda: down().start(), finish_down)], [(start_up, finish_up)]

    def line_stage(self, job, start, size, last):
        n, i = self.n, self.dp
        shard = size // n
        per_side = n if last else n - 1
        base, place, y = self.take(2 * per_side, (2 * n + 1 if last else n + 1) * shard, 0 if last else 2)
        right = {"dp": jnp.minimum(i + 1, n - 1)}
        left = {"dp": jnp.maximum(i - 1, 0)}

        def part(j):
            return self.view(job, start + j * shard, shard)

        def op(s, going_up):
            k = base + 2 * (s + 1 if going_up and last and s == n - 2 else s)
            if going_up:
                send_r, send_l, take_r, take_l = i - s, i + s, i - 1 - s, i + 1 + s
                ok_sr, ok_sl = (i <= n - 2) & (send_r >= 0), (i >= 1) & (send_l <= n - 1)
                ok_tr, ok_tl = (i >= 1) & (take_r >= 0), (i <= n - 2) & (take_l <= n - 1)
            else:
                send_r, send_l, take_r, take_l = n - 1 - s + i, s + i - n + 1, n - 2 - s + i, s + i - n + 2
                ok_sr, ok_sl = (i <= n - 2) & (i <= s), (i >= 1) & (i >= n - 1 - s)
                ok_tr, ok_tl = (i >= 1) & (i - 1 <= s), (i <= n - 2) & (i >= n - 2 - s)

            def there(j, from_right):
                if going_up:
                    return self.landing(job, place + (n + 1 + j) * shard, shard) if last else part(j)
                slot = n if from_right and s == n - 2 else j
                return self.landing(job, place + slot * shard, shard)

            def to_right(j):
                return self.copy(job, k, part(j), there(j, False), right, 0)

            def to_left(j):
                return self.copy(job, k + 1, part(j), there(j, True), left, 1)

            def begin():
                if going_up and not last and s == 0:
                    pl.when(i >= 1)(lambda: pl.semaphore_wait(self.ack(job, y), 1))
                    pl.when(i <= n - 2)(lambda: pl.semaphore_wait(self.ack(job, y + 1), 1))
                pl.when(ok_sr)(lambda: to_right(send_r).start())
                pl.when(ok_sl)(lambda: to_left(send_l).start())

            def finish():
                def took(copy, j, slot):
                    copy.wait_recv()
                    if not going_up:
                        self.combine(job, start + j * shard, place + slot * shard, shard, True)
                    elif last:
                        self.combine(job, start + j * shard, place + (n + 1 + j) * shard, shard, False)

                pl.when(ok_tr)(lambda: took(to_right(take_r), take_r, take_r))
                pl.when(ok_tl)(lambda: took(to_left(take_l), take_l, n if s == n - 2 else take_l))
                pl.when(ok_sr)(lambda: to_right(send_r).wait_send())
                pl.when(ok_sl)(lambda: to_left(send_l).wait_send())
                if not going_up and not last and s == n - 2:
                    pl.when(i <= n - 2)(lambda: self.signal(job, y, right))
                    pl.when(i >= 1)(lambda: self.signal(job, y + 1, left))

            return begin, finish

        return start + i * shard, shard, [op(s, False) for s in range(n - 1)], [op(s, True) for s in range(n - 1)]

    def peer_block(self, o):
        return pltpu.make_async_remote_copy(
            self.G.at[BLOCKS + o % 2],
            self.peer_buf.at[o],
            self.peer_send.at[o],
            self.peer_recv.at[o],
            device_id={"section": 1 - self.sec},
            device_id_type=MESH,
        )

    def fetch(self, o):
        return pltpu.make_async_copy(self.peer_buf.at[o], self.ST, self.load.at[0])

    def result(self, o, dst, remote):
        if remote:
            return pltpu.make_async_remote_copy(
                self.G.at[o],
                dst,
                self.out.at[o],
                self.out_recv.at[o],
                device_id={"section": 1 - self.sec},
                device_id_type=MESH,
            )
        return pltpu.make_async_copy(self.G.at[o], dst, self.out.at[o])

    def output(self, o):
        grad_q, grad_o, grad_i, grad_d = self.outs
        layer, b = 1 - o // OWN, o % OWN * 2 + self.sec

        def to(dst):
            pl.when(layer == self.sec)(lambda: self.result(o, dst, False).start())
            pl.when(layer != self.sec)(lambda: self.result(o, dst, True).start())

        chunk = pl.ds(pl.multiple_of(b // 2 % CHUNKS * D, D), D)
        third = pl.ds(pl.multiple_of(jnp.maximum(b - QKV, 0) * D, D), D)
        pl.when((b < OUT) & (b % 2 == 0))(lambda: to(grad_d.at[chunk, :]))
        pl.when((b < OUT) & (b % 2 == 1))(lambda: to(grad_i.at[:, chunk]))
        pl.when(b == OUT)(lambda: to(grad_o))
        pl.when(b > OUT)(lambda: to(grad_q.at[:, third]))

    def wait_output(self, o):
        grad_o = self.outs[1]
        layer = 1 - o // OWN

        @pl.when(layer == self.sec)
        def _():
            self.result(o, grad_o, False).wait()
            self.result(o, grad_o, True).wait_recv()

        @pl.when(layer != self.sec)
        def _():
            self.result(o, grad_o, True).wait_send()

    def step(self, o, k):
        if k == 0:
            self.peer_block(o).wait_recv()
            self.fetch(o).start()
            return
        if k == 1:
            self.fetch(o).wait()
            g, stage = self.G.at[o], self.ST

            def body(i, _):
                rows = pl.ds(pl.multiple_of(i * 48, 48), 48)
                g[rows, :] = g[rows, :] + stage[rows, :]
                return 0

            lax.fori_loop(0, D // 48, body, 0)

        def advance(kind, typ):
            ops = self.plan((o, typ), kind, typ)
            if k >= 2:
                ops[k - 2][1]()
            if k - 1 < len(ops):
                ops[k - 1][0]()

        advance(0, jnp.int32(0))

        def rest(typ, _):
            advance(1, typ)
            return 0

        lax.fori_loop(1, 3, rest, 0)
        if k == self.steps - 1:
            self.output(o)

    def slot(self, t):
        for k in reversed(range(self.steps)):
            o, valid = jnp.int32(0), False
            for block, times in enumerate(self.table):
                due = t == times[k]
                o = jnp.where(due, block, o)
                valid = valid | due
            pl.when(valid)(functools.partial(self.step, o, k))

    @property
    def slots(self):
        return self.table[-1][-1] + 1


def backward_kernel(
    dp_size, rep_size,
    cot, segs, wall, xs, qkvs, lses, atts, n1s, nbs, us, n2s, rss, tabs, biases, smalls,
    grad_q, grad_o, grad_i, grad_d, grad_small, ing, peer_buf,
    G, RB, ST, WR, UP, N2, NB, DB, DJ, N1, ATT, QK, U, DAT, DN, TAB, BIAS, RS, LSE, SM, SG, SB, SP,
    wsem, lsem, usem, send, recv, load, out, out_recv, peer_send, peer_recv, gsem, ssend, srecv, sync,
):
    sec = lax.axis_index("section")
    dp = lax.axis_index("dp")
    rep = lax.axis_index("rep")
    peer = {"section": 1 - sec}
    tokens = UP.shape[0]
    sums = Blocks(
        G, RB, ST, peer_buf, (grad_q, grad_o, grad_i, grad_d),
        (send, recv, load, out, out_recv, peer_recv, peer_send, sync), dp, rep, dp_size, rep_size,
    )

    def weight(seq):
        layer, b = 1 - seq // BLOCKS, seq % BLOCKS
        return pltpu.make_async_copy(wall.at[layer, b], WR.at[b % 4], wsem.at[b % 4])

    def u_copy(layer, f):
        return pltpu.make_async_copy(us.at[layer, f], U.at[f % 2], usem.at[f % 2])

    def loads(layer):
        return (
            pltpu.make_async_copy(n2s.at[layer], N2, lsem.at[0]),
            pltpu.make_async_copy(nbs.at[layer], NB, lsem.at[1]),
            pltpu.make_async_copy(n1s.at[layer], N1, lsem.at[2]),
            pltpu.make_async_copy(atts.at[layer], ATT, lsem.at[3]),
            pltpu.make_async_copy(qkvs.at[layer], QK, lsem.at[4]),
            pltpu.make_async_copy(rss.at[layer], RS, lsem.at[5]),
            pltpu.make_async_copy(lses.at[layer], LSE, lsem.at[6]),
            pltpu.make_async_copy(xs.at[layer], N2, lsem.at[7]),
        )

    first = (
        pltpu.make_async_copy(cot.at[sec], UP, lsem.at[8]),
        pltpu.make_async_copy(smalls, SM, lsem.at[9]),
        pltpu.make_async_copy(tabs, TAB, lsem.at[10]),
        pltpu.make_async_copy(biases, BIAS, lsem.at[11]),
    )
    for copy in first:
        copy.start()

    barrier = pltpu.get_barrier_semaphore()
    partners = [(peer, None)]
    partners += [({"rep": rep ^ (1 << b)}, None) for b in range(rep_size.bit_length() - 1)]
    partners += [({"dp": dp ^ (1 << b)}, None) for b in range(dp_size.bit_length() - 1)]
    if sums.line:
        partners += [({"dp": jnp.minimum(dp + 1, dp_size - 1)}, dp < dp_size - 1)]
        partners += [({"dp": jnp.maximum(dp - 1, 0)}, dp > 0)]
    count = 0
    for device, valid in partners:

        def greet(device=device):
            pl.semaphore_signal(barrier, inc=1, device_id=device, device_id_type=MESH)

        if valid is None:
            greet()
            count = count + 1
        else:
            pl.when(valid)(greet)
            count = count + jnp.where(valid, 1, 0)
    pl.semaphore_wait(barrier, count)

    for seq in range(4):
        weight(seq).start()
    real = jnp.where(own_segments(segs, sec)[1] < SLOT // MINLEN, 1.0, 0.0).astype(F32)

    def in_copies(layer):
        mine = pltpu.make_async_copy(UP, ing.at[sec], gsem.at[0])
        theirs = pltpu.make_async_remote_copy(
            UP, ing.at[sec], gsem.at[1], gsem.at[2], device_id=peer, device_id_type=MESH
        )
        return mine, theirs

    def layer_step(li, _):
        layer = 1 - li
        copies = loads(layer)
        for copy in copies[:7]:
            copy.start()
        u_copy(layer, 0).start()
        u_copy(layer, 1).start()

        def slot(s):
            sums.slot(li * CALLS + s)

        def outer(lhs, rhs, b):
            o = li * OWN + b // 2
            mine = b % 2 == sec

            @pl.when(~mine & (o >= 2))
            def _():
                sums.peer_block(o - 2).wait_send()

            t = jnp.where(mine, o, BLOCKS + o % 2)
            for c in range(3):
                cols = slice(c * 256, (c + 1) * 256)
                G[t, :, cols] = dot_tn(lhs[...], rhs[:, cols]).astype(BF16)

            pl.when(~mine)(lambda: sums.peer_block(o).start())

        @pl.when(li == 0)
        def _():
            for copy in first:
                copy.wait()
            UP[...] = (UP[...].astype(F32) * real).astype(BF16)

        copies[0].wait()
        copies[5].wait()

        def norm_back(grad, n, gain, scale):
            a = grad * gain
            m1 = jnp.mean(a, axis=1, keepdims=True)
            m2 = jnp.mean(a * n, axis=1, keepdims=True)
            return (a - m1 - n * m2) * scale

        def rows_sum(value):
            return jnp.sum(value, axis=0, keepdims=True)

        for row in (G_FFN, B_FFN, B_DOWN, G_ATTN, B_ATTN, B_OUT):
            SG[layer, row] = jnp.zeros((1, D), F32)
        for row in (13, 14, 15):
            SG[layer, row] = jnp.zeros((1, D), F32)

        def second_norm(c, _):
            rows = pl.ds(pl.multiple_of(c * 256, 256), 256)
            up = UP[rows, :].astype(F32)
            n = N2[rows, :].astype(F32)
            scale = RS[1, rows, 0:1]
            g = norm_back(up, n, SM[layer, G_FFN], scale)
            DN[rows, :] = g
            DB[rows, :] = g.astype(BF16)
            SG[layer, G_FFN] += rows_sum(up * n)
            SG[layer, B_FFN] += rows_sum(up)
            SG[layer, B_DOWN] += rows_sum(g)
            return 0

        lax.fori_loop(0, tokens // 256, second_norm, 0)
        copies[7].start()
        copies[1].wait()

        def ffn(f, _):
            u_copy(layer, f).wait()
            weight(li * BLOCKS + 2 * f).wait()
            weight(li * BLOCKS + 2 * f + 1).wait()
            down, up = WR.at[2 * f % 4], WR.at[(2 * f + 1) % 4]
            for c in range(3):
                cols = slice(c * 256, (c + 1) * 256)
                u = U[f % 2, :, cols].astype(F32)
                square, t = gelu_parts(u)
                lift = 1.0 + t
                DJ[1, :, cols] = (0.5 * u * lift).astype(BF16)
                slope = 0.5 * lift * (1.0 + u * (1.0 - t) * (GELU_A * (1.0 + 3.0 * GELU_B * square)))
                grad = dot_t(DB[...], down[cols, :]) * slope
                SG[layer, B_IN + f, :, cols] = rows_sum(grad)
                DJ[0, :, cols] = grad.astype(BF16)
            outer(DJ.at[1], DB, 2 * f)
            slot(2 * f)
            outer(NB, DJ.at[0], 2 * f + 1)
            for c in range(3):
                cols = slice(c * 256, (c + 1) * 256)
                DN[:, cols] += dot_t(DJ[0], up[cols, :])
            weight(li * BLOCKS + 2 * f + 4).start()
            weight(li * BLOCKS + 2 * f + 5).start()
            pl.when(f + 2 < CHUNKS)(lambda: u_copy(layer, f + 2).start())
            slot(2 * f + 1)
            return 0

        lax.fori_loop(0, CHUNKS, ffn, 0)
        copies[2].wait()

        def first_norm(c, _):
            rows = pl.ds(pl.multiple_of(c * 256, 256), 256)
            up = DN[rows, :]
            n = N1[rows, :].astype(F32)
            g = norm_back(up, n, SM[layer, G_ATTN], RS[0, rows, 0:1])
            DN[rows, :] = g
            DB[rows, :] = g.astype(BF16)
            SG[layer, G_ATTN] += rows_sum(up * n)
            SG[layer, B_ATTN] += rows_sum(up)
            SG[layer, B_OUT] += rows_sum(g)
            return 0

        lax.fori_loop(0, tokens // 256, first_norm, 0)
        copies[3].wait()
        outer(ATT, DB, OUT)
        weight(li * BLOCKS + OUT).wait()
        w_out = WR.at[OUT % 4]
        for c in range(3):
            cols = slice(c * 256, (c + 1) * 256)
            DAT[:, cols] = dot_t(DB[...], w_out[cols, :]).astype(BF16)
        pl.when(li == 0)(lambda: weight(BLOCKS).start())
        slot(2 * CHUNKS)
        copies[4].wait()
        copies[6].wait()

        def pair(hp, _):
            lanes = pl.ds(pl.multiple_of(hp * 128, 128), 128)
            q2 = QK[0, :, lanes]
            k2 = QK[1, :, lanes]
            v2 = QK[2, :, lanes]
            o2 = DAT[:, lanes]
            low = low_lanes(k2.shape)
            k_t = k2.T
            zero = jnp.zeros_like(k2)
            grads_q, grads_k, grads_v = [], [], []
            for h in range(2):
                mask = low if h == 0 else ~low
                s = dot_t(jnp.where(mask, k2, zero), q2) * SCORE + BIAS[...]
                p = jnp.exp2(s - LSE[hp, h : h + 1, :])
                dprob = dot_t(jnp.where(mask, v2, zero), o2)
                inner = jnp.sum(p * dprob, axis=0, keepdims=True)
                ds = (p * (dprob - inner)).astype(BF16)
                grads_v.append(dot(p.astype(BF16), o2))
                grads_k.append(dot(ds, q2))
                grads_q.append(dot(k_t[h * HEAD : (h + 1) * HEAD], ds))
            scale = 1.0 / math.sqrt(HEAD)
            gq = jnp.concatenate(grads_q, axis=0).T * scale
            gk = jnp.where(low, grads_k[0], grads_k[1]) * scale
            gv = jnp.where(low, grads_v[0], grads_v[1])
            cos, sin = TAB[0], TAB[1]
            gq = gq * cos - swap_halves(gq) * sin
            gk = gk * cos - swap_halves(gk) * sin
            for third, g in enumerate((gq, gk, gv)):
                DJ[third, :, lanes] = g.astype(BF16)
                SG[layer, B_QKV + third, :, lanes] = rows_sum(g)
            slot(2 * CHUNKS + 1 + hp)
            return 0

        lax.fori_loop(0, PAIRS, pair, 0)
        copies[7].wait()

        def third_step(third, _):
            outer(N2, DJ.at[third], QKV + third)
            weight(li * BLOCKS + QKV + third).wait()
            w = WR.at[(QKV + third) % 4]
            for c in range(3):
                cols = slice(c * 256, (c + 1) * 256)
                DN[:, cols] += dot_t(DJ[third], w[cols, :])
            pl.when(li == 0)(lambda: weight(BLOCKS + 1 + third).start())
            slot(CALLS - 3 + third)
            return 0

        lax.fori_loop(0, 3, third_step, 0)

        mine, theirs = in_copies(layer)
        @pl.when(li == 1)
        def _():
            pl.when(sec == 1)(lambda: mine.wait())
            pl.when(sec == 0)(lambda: theirs.wait_send())

        UP[...] = DN[...].astype(BF16)
        pl.when(layer == sec)(lambda: mine.start())
        pl.when(layer != sec)(lambda: theirs.start())
        return 0

    lax.fori_loop(0, 2, layer_step, 0)

    small_partners = [peer] + [device for device, valid in partners[1:] if valid is None]

    def small_copy(m):
        src = SG.at[1 - sec] if m == 0 else SP.at[m - 1]
        return pltpu.make_async_remote_copy(
            src, SB.at[m], ssend.at[m], srecv.at[m], device_id=small_partners[m], device_id_type=MESH
        )

    small_copy(0).start()

    def small_step(m):
        small_copy(m).wait_recv()
        SP[m] = (SG[sec] if m == 0 else SP[m - 1]) + SB[m]
        if m + 1 < len(small_partners):
            small_copy(m + 1).start()

    rounds = max(sums.slots - 2 * CALLS, len(small_partners))

    def final(i, _):
        sums.slot(2 * CALLS + i)
        for m in range(len(small_partners)):
            pl.when(i == m)(functools.partial(small_step, m))
        return 0

    lax.fori_loop(0, rounds, final, 0)
    for m in range(len(small_partners)):
        small_copy(m).wait_send()
    small_out = pltpu.make_async_copy(SP.at[len(small_partners) - 1], grad_small, ssend.at[0])
    small_out.start()

    for o in (BLOCKS - 2, BLOCKS - 1):
        sums.peer_block(o).wait_send()

    def out_wait(o, _):
        sums.wait_output(o)
        return 0

    lax.fori_loop(0, BLOCKS, out_wait, 0)
    small_out.wait()
    mine, theirs = in_copies(0)
    pl.when(sec == 0)(lambda: mine.wait())
    pl.when(sec == 1)(lambda: theirs.wait_send())
    theirs.wait_recv()


RING = 6
ROWS = 256


def convert_kernel(
    grad_q, grad_o, grad_i, grad_d, small,
    out_q, out_o, out_i, out_d, b_q, b_o, g_a, b_a, b_i, b_d, g_f, b_f,
    LOW, HIGH, isem, osem,
):
    tiles = []
    for src, dst in ((grad_q, out_q), (grad_o, out_o), (grad_i, out_i), (grad_d, out_d)):
        for r in range(src.shape[0] // ROWS):
            for c in range(src.shape[1] // D):
                part = (pl.ds(r * ROWS, ROWS), pl.ds(c * D, D))
                tiles.append((src.at[part], dst.at[0, part[0], part[1]]))
    reads = [pltpu.make_async_copy(src, LOW.at[i % RING], isem.at[i % RING]) for i, (src, _) in enumerate(tiles)]
    writes = [pltpu.make_async_copy(HIGH.at[i % RING], dst, osem.at[i % RING]) for i, (_, dst) in enumerate(tiles)]
    for i in range(RING):
        reads[i].start()
    for row, ref in ((B_QKV, b_q), (B_OUT, b_o), (G_ATTN, g_a), (B_ATTN, b_a), (B_IN, b_i), (B_DOWN, b_d), (G_FFN, g_f), (B_FFN, b_f)):
        for i in range(ref.shape[1] // D):
            ref[0:1, i * D : (i + 1) * D] = small[row + i]
    for i in range(len(tiles)):
        reads[i].wait()
        if i >= RING:
            writes[i - RING].wait()

        def body(r, _, at=i % RING):
            rows = pl.ds(pl.multiple_of(r * 64, 64), 64)
            HIGH[at, rows, :] = LOW[at, rows, :].astype(F32)
            return 0

        lax.fori_loop(0, ROWS // 64, body, 0)
        writes[i].start()
        if i + RING < len(tiles):
            reads[i + RING].start()
    for write in writes[len(tiles) - RING :]:
        write.wait()


def per_device(
    dp_size, rep_size, inputs, segments, cotangent, w_qkv, b_qkv, w_out, b_out, g_attn, b_attn, w_in, b_in, w_down,
    b_down, g_ffn, b_ffn,
):
    tokens = inputs.shape[1]
    anywhere = pl.BlockSpec(memory_space=pl.ANY)
    in_vmem = pl.BlockSpec(memory_space=pltpu.VMEM)

    def shape(*dims, dtype=BF16):
        return jax.ShapeDtypeStruct(dims, dtype)

    def mem(*dims, dtype=BF16):
        return pltpu.VMEM(dims, dtype)

    dma = pltpu.SemaphoreType.DMA
    stash = pl.pallas_call(
        forward_kernel,
        out_shape=(
            shape(2, BLOCKS, D, D),
            shape(2, tokens, D),
            shape(2, 3, tokens, D),
            shape(2, PAIRS, 8, tokens, dtype=F32),
            shape(2, tokens, D),
            shape(2, tokens, D),
            shape(2, tokens, D),
            shape(2, CHUNKS, tokens, D),
            shape(2, tokens, D),
            shape(2, 2, tokens, 128, dtype=F32),
            shape(2, tokens, 128, dtype=F32),
            shape(tokens, tokens, dtype=F32),
            shape(2, tokens, D),
            shape(2, SMALL, 1, D, dtype=F32),
        ),
        in_specs=[anywhere, in_vmem] + [anywhere] * 4 + [in_vmem] * 8,
        out_specs=(anywhere,) * 14,
        scratch_shapes=[
            mem(2, BLOCKS, D, D),
            mem(2, SMALL, 1, D, dtype=F32),
            mem(3, tokens, D),
            mem(2, 3, tokens, D),
            mem(2, PAIRS, 8, tokens, dtype=F32),
            mem(2, tokens, D),
            mem(2, tokens, D),
            mem(2, tokens, D),
            mem(2, CHUNKS, tokens, D),
            mem(2, tokens, D),
            mem(2, 2, tokens, 128, dtype=F32),
            mem(2, tokens, 128, dtype=F32),
            mem(tokens, tokens, dtype=F32),
            mem(tokens, D, dtype=F32),
            mem(tokens, D),
            dma((BLOCKS,)),
            dma((BLOCKS,)),
            dma((BLOCKS,)),
            dma((6,)),
            dma((2, BLOCKS)),
            dma((2, 9)),
            dma((3,)),
        ],
        compiler_params=pltpu.CompilerParams(collective_id=0, has_side_effects=True, vmem_limit_bytes=VMEM_LIMIT),
        name="forward",
    )(inputs, segments, w_qkv, w_out, w_in, w_down, b_qkv, b_out, g_attn, b_attn, b_in, b_down, g_ffn, b_ffn)
    (wall, xs, qkvs, lses, atts, n1s, nbs, us, n2s, rss, tabs, biases, acts, smalls) = stash

    line = dp_size == 4 and rep_size == 4
    bits = dp_size.bit_length() + rep_size.bit_length() - 2
    ring = BLOCKS
    landing = 1152 if line else 912
    out = pl.pallas_call(
        functools.partial(backward_kernel, dp_size, rep_size),
        out_shape=(
            shape(D, 3 * D),
            shape(D, D),
            shape(D, CHUNKS * D),
            shape(CHUNKS * D, D),
            shape(SMALL, 1, D, dtype=F32),
            shape(2, tokens, D),
            shape(BLOCKS, D, D),
        ),
        in_specs=[anywhere, in_vmem] + [anywhere] * 13,
        out_specs=(anywhere,) * 7,
        scratch_shapes=[
            mem(BLOCKS + 2, D, D),
            mem(ring, 3, landing, THIRD),
            mem(D, D),
            mem(4, D, D),
            mem(tokens, D),
            mem(tokens, D),
            mem(tokens, D),
            mem(tokens, D),
            mem(3, tokens, D),
            mem(tokens, D),
            mem(tokens, D),
            mem(3, tokens, D),
            mem(2, tokens, D),
            mem(tokens, D),
            mem(tokens, D, dtype=F32),
            mem(2, tokens, 128, dtype=F32),
            mem(tokens, tokens, dtype=F32),
            mem(2, tokens, 128, dtype=F32),
            mem(PAIRS, 8, tokens, dtype=F32),
            mem(2, SMALL, 1, D, dtype=F32),
            mem(2, SMALL, 1, D, dtype=F32),
            mem(bits + 1, SMALL, 1, D, dtype=F32),
            mem(bits + 1, SMALL, 1, D, dtype=F32),
            dma((4,)),
            dma((12,)),
            dma((2,)),
            dma((3 * ring, 2)),
            dma((3 * ring, 10)),
            dma((1,)),
            dma((BLOCKS,)),
            dma((BLOCKS,)),
            dma((BLOCKS,)),
            dma((BLOCKS,)),
            dma((3,)),
            dma((bits + 1,)),
            dma((bits + 1,)),
            pltpu.SemaphoreType.REGULAR((3 * ring, 3)),
        ],
        compiler_params=pltpu.CompilerParams(collective_id=1, has_side_effects=True, vmem_limit_bytes=VMEM_LIMIT),
        name="backward",
    )(cotangent, segments, wall, xs, qkvs, lses, atts, n1s, nbs, us, n2s, rss, tabs, biases, smalls)
    grad_q, grad_o, grad_i, grad_d, grad_small, ing, _ = out
    vectors = (3 * D, D, D, D, CHUNKS * D, D, D, D)
    grads = pl.pallas_call(
        convert_kernel,
        out_shape=(
            *(shape(1, *grad.shape, dtype=F32) for grad in (grad_q, grad_o, grad_i, grad_d)),
            *(shape(1, size, dtype=F32) for size in vectors),
        ),
        in_specs=[anywhere] * 4 + [in_vmem],
        out_specs=(anywhere,) * 4 + (in_vmem,) * 8,
        scratch_shapes=[
            mem(RING, ROWS, D),
            mem(RING, ROWS, D, dtype=F32),
            dma((RING,)),
            dma((RING,)),
        ],
        compiler_params=pltpu.CompilerParams(vmem_limit_bytes=VMEM_LIMIT),
        name="convert",
    )(grad_q, grad_o, grad_i, grad_d, grad_small)
    grad_q, grad_o, grad_i, grad_d, b_q, b_o, g_a, b_a, b_i, b_d, g_f, b_f = grads
    return acts[None], ing[None], grad_q, b_q, grad_o, b_o, g_a, b_a, grad_i, b_i, grad_d, b_d, g_f, b_f


def solution(mesh):
    tokens = ("dp", "rep")
    weight, vector = P("section", None, None), P("section", None)
    weights = (weight, vector, weight, vector, vector, vector, weight, vector, weight, vector, vector, vector)
    activations = P("section", None, tokens, None)
    return jax.shard_map(
        functools.partial(per_device, mesh.shape["dp"], mesh.shape["rep"]),
        mesh=mesh,
        in_specs=(P(None, tokens, None), P(None, tokens), P(None, tokens, None), *weights),
        out_specs=(activations, activations, *weights),
        check_vma=False,
    )
```

```python
import functools
import math

import jax
import jax.numpy as jnp
from jax import lax
from jax.experimental import pallas as pl
from jax.experimental.pallas import tpu as pltpu
from jax.sharding import PartitionSpec as P

D = 768
HEADS = 12
HEAD = 64
PAIRS = HEADS // 2
SLOT = 512
MINLEN = 64
CHUNKS = 4
OUT = 2 * CHUNKS
QKV = OUT + 1
BLOCKS = QKV + 3
SEND_ORDER = (9, 10, 11, 8, 1, 0, 3, 2, 5, 4, 7, 6)
B_QKV, B_OUT, G_ATTN, B_ATTN, B_IN, B_DOWN, G_FFN, B_FFN = 0, 3, 4, 5, 6, 10, 11, 12
SMALL = 16
EPSILON = 1e-05
NEG_LARGE = -1e30
LOG2E = math.log2(math.e)
SCORE = LOG2E / math.sqrt(HEAD)
GELU_A = math.sqrt(2.0 / math.pi)
GELU_B = 0.044715
THIRD = D // 3
OWN = BLOCKS // 2
CALLS = 18
FINAL = 2 * CALLS
TABLE = (
    (1, 2, 5, 8, 11, 14, 16, 18, 21, 24, 27, 30),
    (3, 4, 7, 10, 13, 16, 18, 20, 23, 26, 29, 32),
    (5, 6, 9, 12, 15, 18, 20, 22, 25, 28, 31, 34),
    (7, 8, 11, 14, 17, 20, 22, 24, 27, 30, 33, 36),
    (15, 16, 19, 22, 25, 28, 30, 32, 35, 36, 37, 38),
    (17, 18, 21, 24, 27, 30, 32, 34, 36, 37, 38, 39),
    (19, 20, 23, 26, 29, 32, 34, 36, 37, 38, 39, 40),
    (21, 22, 25, 28, 31, 34, 36, 37, 38, 39, 40, 41),
    (23, 24, 27, 30, 33, 36, 37, 38, 39, 40, 41, 42),
    (25, 26, 29, 32, 35, 37, 38, 39, 40, 41, 42, 43),
    (33, 34, 36, 37, 38, 39, 40, 41, 42, 43, 44, 45),
    (35, 36, 37, 38, 39, 40, 41, 42, 43, 44, 45, 46),
)


def timetable(steps):
    ready = [CALLS * li + at for li in range(2) for at in (1, 3, 5, 7, 15, 17)]
    table = []
    for o, first in enumerate(ready):
        times = []
        for k in range(steps):
            t = max(first, times[-1] + 1 if k else 0, table[-1][k] + 1 if o else 0)
            times.append(t)
        table.append(times)
    return table


MESH = pl.DeviceIdType.MESH
F32 = jnp.float32
BF16 = jnp.bfloat16
VMEM_LIMIT = 62 * 1024 * 1024


def dot(a, b):
    return lax.dot_general(a, b, (((1,), (0,)), ((), ())), preferred_element_type=F32)


def dot_t(a, b):
    return lax.dot_general(a, b, (((1,), (1,)), ((), ())), preferred_element_type=F32)


def dot_tn(a, b):
    return lax.dot_general(a, b, (((0,), (0,)), ((), ())), preferred_element_type=F32)


def swap_halves(t):
    lane = lax.broadcasted_iota(jnp.int32, t.shape, 1)
    return jnp.where(lane % HEAD < HEAD // 2, pltpu.roll(t, 96, 1), pltpu.roll(t, 32, 1))


def low_lanes(shape):
    return lax.broadcasted_iota(jnp.int32, shape, 1) < HEAD


def own_segments(segs, sec):
    row = jnp.where(sec == 0, segs[0:1, :], segs[1:2, :]).astype(F32)
    return row, jnp.broadcast_to(row, (128, row.shape[1])).T[:, 0:1]


def gelu_parts(u):
    square = u * u
    t = jnp.tanh(GELU_A * u * (1.0 + GELU_B * square))
    return square, t


def forward_kernel(
    inp, segs, wq, wo, wi, wd, bq, bo, ga, ba, bi, bd, gf, bf,
    wall, xs, qkvs, lses, atts, n1s, nbs, us, n2s, rss, tabs, biases, acts, smalls,
    W, SM, X, QK, LSE, ATT, N1, NB, U, N2, RS, TAB, BIAS, ACC, ACT,
    osem, rsend, rrecv, ssem, wsem, stash, asem,
):
    sec = lax.axis_index("section")
    other = 1 - sec
    peer = {"section": other}
    tokens = X.shape[1]

    def source(b):
        if b < OUT:
            part = pl.ds(b // 2 * D, D)
            return wd.at[0, part, :] if b % 2 == 0 else wi.at[0, :, part]
        if b == OUT:
            return wo.at[0]
        return wq.at[0, :, pl.ds((b - QKV) * D, D)]

    def own_copy(b):
        return pltpu.make_async_copy(source(b), W.at[sec, b], osem.at[b])

    def peer_copy(b):
        return pltpu.make_async_remote_copy(
            source(b), W.at[sec, b], rsend.at[b], rrecv.at[b], device_id=peer, device_id_type=MESH
        )

    load_x = pltpu.make_async_copy(inp.at[sec], X.at[0], ssem.at[0])
    load_x.start()
    for b in SEND_ORDER[:4]:
        own_copy(b).start()
    barrier = pltpu.get_barrier_semaphore()
    pl.semaphore_signal(barrier, inc=1, device_id=peer, device_id_type=MESH)
    pl.semaphore_wait(barrier, 1)
    for row, ref in ((B_QKV, bq), (B_OUT, bo), (G_ATTN, ga), (B_ATTN, ba), (B_IN, bi), (B_DOWN, bd), (G_FFN, gf), (B_FFN, bf)):
        for i in range(ref.shape[1] // D):
            SM[sec, row + i] = ref[0:1, i * D : (i + 1) * D].astype(F32)
    for row in range(B_FFN + 1, SMALL):
        SM[sec, row] = jnp.zeros((1, D), F32)
    small_copy = pltpu.make_async_remote_copy(
        SM.at[sec], SM.at[sec], ssem.at[1], ssem.at[2], device_id=peer, device_id_type=MESH
    )
    small_copy.start()
    for b in SEND_ORDER:
        peer_copy(b).start()
    for b in SEND_ORDER[4:]:
        own_copy(b).start()

    row_at = lax.broadcasted_iota(jnp.int32, (tokens, tokens), 0)
    col_at = lax.broadcasted_iota(jnp.int32, (tokens, tokens), 1)
    seg_row, seg_col = own_segments(segs, sec)
    same = seg_col == seg_row
    position = jnp.sum(jnp.where(same & (col_at < row_at), 1.0, 0.0), axis=1, keepdims=True)
    allowed = (same & (seg_col < SLOT // MINLEN)) | (row_at == col_at)
    BIAS[...] = jnp.where(allowed, 0.0, NEG_LARGE)
    lane = lax.broadcasted_iota(jnp.int32, (1, 128), 1)
    frequency = jnp.exp((lane % 32).astype(F32) * (-2.0 * math.log(10000.0) / HEAD))
    angle = position * frequency
    TAB[0] = jnp.cos(angle)
    sine = jnp.sin(angle)
    TAB[1] = jnp.where(lane % HEAD < HEAD // 2, -sine, sine)
    table_out = pltpu.make_async_copy(TAB, tabs, ssem.at[3])
    table_out.start()
    bias_out = pltpu.make_async_copy(BIAS, biases, ssem.at[4])
    bias_out.start()
    load_x.wait()
    small_copy.wait()
    small_out = pltpu.make_async_copy(SM, smalls, ssem.at[5])
    small_out.start()

    def keep(k, layer, src, dst):
        pltpu.make_async_copy(src.at[layer], dst.at[layer], stash.at[layer, k]).start()

    def layer_step(layer, _):
        def ready(b):
            @pl.when(layer == sec)
            def _():
                pltpu.make_async_copy(wo.at[0], W.at[sec, b], osem.at[b]).wait()

            @pl.when(layer != sec)
            def _():
                pltpu.make_async_remote_copy(
                    wo.at[0], W.at[other, b], rsend.at[b], rrecv.at[b], device_id=peer, device_id_type=MESH
                ).wait_recv()

            pltpu.make_async_copy(W.at[layer, b], wall.at[layer, b], wsem.at[layer, b]).start()

        keep(0, layer, X, xs)
        for third in range(3):
            ready(QKV + third)

            for c in range(3):
                cols = slice(c * 256, (c + 1) * 256)
                joined = dot(X[layer], W[layer, QKV + third, :, cols]) + SM[layer, B_QKV + third, :, cols]
                if third == 2:
                    QK[layer, third, :, cols] = joined.astype(BF16)
                else:
                    parts = []
                    for h in range(2):
                        t = joined[:, h * 128 : (h + 1) * 128]
                        parts.append((t * TAB[0] + swap_halves(t) * TAB[1]).astype(BF16))
                    QK[layer, third, :, cols] = jnp.concatenate(parts, axis=1)
        keep(1, layer, QK, qkvs)

        def pair(hp, _):
            lanes = pl.ds(pl.multiple_of(hp * 128, 128), 128)
            q2 = QK[layer, 0, :, lanes]
            k2 = QK[layer, 1, :, lanes]
            v_t = QK[layer, 2, :, lanes].T
            low = low_lanes(k2.shape)
            outs = []
            for h in range(2):
                k_one = jnp.where(low if h == 0 else ~low, k2, jnp.zeros_like(k2))
                s = dot_t(k_one, q2) * SCORE + BIAS[...]
                peak = jnp.max(s, axis=0, keepdims=True)
                p = jnp.exp2(s - peak)
                total = jnp.sum(p, axis=0, keepdims=True)
                LSE[layer, hp, h : h + 1, :] = peak + jnp.log(total) * LOG2E
                outs.append(dot(v_t[h * HEAD : (h + 1) * HEAD], p.astype(BF16)) * (1.0 / total))
            ATT[layer, :, lanes] = jnp.concatenate(outs, axis=0).T.astype(BF16)
            return 0

        lax.fori_loop(0, PAIRS, pair, 0, unroll=3)
        keep(2, layer, LSE, lses)
        keep(3, layer, ATT, atts)
        ready(OUT)

        def norm_rows(r):
            mean = jnp.mean(r, axis=1, keepdims=True)
            centered = r - mean
            scale = lax.rsqrt(jnp.mean(centered * centered, axis=1, keepdims=True) + EPSILON)
            return centered * scale, scale

        def first_norm(c, _):
            rows = pl.ds(pl.multiple_of(c * 256, 256), 256)
            r = X[layer, rows, :].astype(F32) + dot(ATT[layer, rows, :], W[layer, OUT]) + SM[layer, B_OUT]
            n, scale = norm_rows(r)
            N1[layer, rows, :] = n.astype(BF16)
            RS[layer, 0, rows, :] = jnp.broadcast_to(scale, (256, 128))
            y = n * SM[layer, G_ATTN] + SM[layer, B_ATTN]
            NB[layer, rows, :] = y.astype(BF16)
            ACC[rows, :] = y + SM[layer, B_DOWN]
            return 0

        lax.fori_loop(0, tokens // 256, first_norm, 0, unroll=2)
        keep(4, layer, N1, n1s)
        keep(5, layer, NB, nbs)

        def ffn(f, _):
            ready(2 * f + 1)

            for c in range(3):
                cols = slice(c * 256, (c + 1) * 256)
                u = dot(NB[layer], W[layer, 2 * f + 1, :, cols]) + SM[layer, B_IN + f, :, cols]
                U[layer, f, :, cols] = u.astype(BF16)
                ACT[:, cols] = (0.5 * u * (1.0 + gelu_parts(u)[1])).astype(BF16)
            ready(2 * f)
            for c in range(3):
                cols = slice(c * 256, (c + 1) * 256)
                ACC[:, cols] += dot(ACT[...], W[layer, 2 * f, :, cols])
            return 0

        lax.fori_loop(0, CHUNKS, ffn, 0, unroll=2)
        keep(6, layer, U, us)

        def second_norm(c, _):
            rows = pl.ds(pl.multiple_of(c * 256, 256), 256)
            n, scale = norm_rows(ACC[rows, :])
            N2[layer, rows, :] = n.astype(BF16)
            RS[layer, 1, rows, :] = jnp.broadcast_to(scale, (256, 128))
            X[layer + 1, rows, :] = (n * SM[layer, G_FFN] + SM[layer, B_FFN]).astype(BF16)
            return 0

        lax.fori_loop(0, tokens // 256, second_norm, 0, unroll=2)
        keep(7, layer, N2, n2s)
        keep(8, layer, RS, rss)

        @pl.when(layer == sec)
        def _():
            pltpu.make_async_copy(X.at[layer + 1], acts.at[sec], asem.at[0]).start()

        @pl.when(layer != sec)
        def _():
            pltpu.make_async_remote_copy(
                X.at[layer + 1], acts.at[sec], asem.at[1], asem.at[2], device_id=peer, device_id_type=MESH
            ).start()

        return 0

    lax.fori_loop(0, 2, layer_step, 0)

    table_out.wait()
    bias_out.wait()
    small_out.wait()

    def finish(layer, _):
        for k, (src, dst) in enumerate(
            ((X, xs), (QK, qkvs), (LSE, lses), (ATT, atts), (N1, n1s), (NB, nbs), (U, us), (N2, n2s), (RS, rss))
        ):
            pltpu.make_async_copy(src.at[layer], dst.at[layer], stash.at[layer, k]).wait()
        for b in range(BLOCKS):
            pltpu.make_async_copy(W.at[layer, b], wall.at[layer, b], wsem.at[layer, b]).wait()
        return 0

    lax.fori_loop(0, 2, finish, 0)
    for b in range(BLOCKS):
        peer_copy(b).wait_send()
    pltpu.make_async_copy(X.at[1], acts.at[sec], asem.at[0]).wait()
    last = pltpu.make_async_remote_copy(
        X.at[1], acts.at[sec], asem.at[1], asem.at[2], device_id=peer, device_id_type=MESH
    )
    last.wait_send()
    last.wait_recv()


class Blocks:
    def __init__(self, G, RB, ST, peer_buf, outs, sems, dp, rep, dp_size, rep_size):
        self.G, self.RB, self.ST, self.peer_buf, self.outs = G, RB, ST, peer_buf, outs
        (self.send, self.recv, self.load, self.out, self.out_recv, self.peer_recv, self.peer_send, self.sync) = sems
        self.sec, self.dp, self.rep, self.n, self.rep_size = lax.axis_index("section"), dp, rep, dp_size, rep_size
        self.line = dp_size == 4 and rep_size == 4
        self.ring = RB.shape[0]
        for kind in (0, 1):
            self.steps = len(self.plan(jnp.int32(0), kind, jnp.int32(kind))) + 2
        self.table = TABLE if self.steps == len(TABLE[0]) else timetable(self.steps)

    def view(self, job, start, size):
        block, typ = job
        return self.G.at[block, typ, pl.ds(pl.multiple_of(start, 16), size), :]

    def landing(self, job, start, size):
        block, typ = job
        return self.RB.at[block % self.ring, typ, pl.ds(pl.multiple_of(start, 16), size), :]

    def copy(self, job, k, src, dst, device, side=0):
        block, typ = job
        slot = block % self.ring * 3 + typ
        return pltpu.make_async_remote_copy(
            src, dst, self.send.at[slot, side], self.recv.at[slot, k], device_id=device, device_id_type=MESH
        )

    def combine(self, job, start, place, size, add):
        step = 96 if size % 96 == 0 else 48
        g = self.view(job, start, size)
        r = self.landing(job, place, size)

        def body(i, _):
            rows = pl.ds(pl.multiple_of(i * step, 16), step)
            g[rows, :] = g[rows, :] + r[rows, :] if add else r[rows, :]
            return 0

        lax.fori_loop(0, size // step, body, 0)

    def plan(self, job, kind, typ):
        if not isinstance(job, tuple):
            job = (job, typ)
        self.sem_at = 0
        self.sync_at = 0
        self.place_at = 0
        if self.line:
            bits = [("rep", typ - 1), ("rep", 2 - typ)] if kind else [("rep", job[0] & 1), ("rep", 1 - (job[0] & 1))]
            stages = bits + ["line"] if kind else ["line"] + bits
        else:
            stages = [("rep", b) for b in range(self.rep_size.bit_length() - 1)]
            stages += [("dp", b) for b in range(self.n.bit_length() - 1)]
        total, size = 0, D
        for stage in stages:
            if stage == "line":
                size //= self.n
                total += 1
            elif self.halves(size):
                size //= 2
                total += 1
        start, size, cuts = jnp.int32(0), D, 0
        down, up = [], []
        for stage in stages:
            if stage == "line":
                cuts += 1
                start, size, a, b = self.line_stage(job, start, size, cuts == total)
            elif self.halves(size):
                cuts += 1
                start, size, a, b = self.pair_stage(job, start, size, *stage, cuts == total)
            else:
                a, b = self.swap_stage(job, start, size, *stage), []
            down = down + a
            up = b + up
        assert self.sem_at <= self.recv.shape[1] and self.place_at <= self.RB.shape[2]
        assert self.sync_at <= self.sync.shape[1]
        return down + up

    @staticmethod
    def halves(size):
        return size // 2 % 48 == 0

    def take(self, sems, rows, syncs=0):
        k, place, y = self.sem_at, self.place_at, self.sync_at
        self.sem_at += sems
        self.place_at += rows
        self.sync_at += syncs
        return k, place, y

    def ack(self, job, y):
        return self.sync.at[job[0] % self.ring * 3 + job[1], y]

    def signal(self, job, y, device):
        pl.semaphore_signal(self.ack(job, y), inc=1, device_id=device, device_id_type=MESH)

    def swap_stage(self, job, start, size, axis, bit):
        index = self.rep if axis == "rep" else self.dp
        device = {axis: index ^ (1 << bit)}
        k, place, _ = self.take(1, size)

        def swap():
            return self.copy(job, k, self.view(job, start, size), self.landing(job, place, size), device)

        def finish():
            swap().wait()
            self.combine(job, start, place, size, True)

        return [(lambda: swap().start(), finish)]

    def pair_stage(self, job, start, size, axis, bit, last):
        index = self.rep if axis == "rep" else self.dp
        mine = (index >> bit) & 1
        device = {axis: index ^ (1 << bit)}
        half = size // 2
        kept, given = start + mine * half, start + (1 - mine) * half
        k, place, y = self.take(2 if last else 1, 2 * half if last else half, 0 if last else 1)

        def down():
            return self.copy(job, k, self.view(job, given, half), self.landing(job, place, half), device)

        def up():
            there = self.landing(job, place + half, half) if last else self.view(job, kept, half)
            return self.copy(job, k + 1 if last else k, self.view(job, kept, half), there, device)

        def finish_down():
            down().wait_recv()
            self.combine(job, kept, place, half, True)
            down().wait_send()
            if not last:
                self.signal(job, y, device)

        def start_up():
            if not last:
                pl.semaphore_wait(self.ack(job, y), 1)
            up().start()

        def finish_up():
            up().wait()
            if last:
                self.combine(job, given, place + half, half, False)

        return kept, half, [(lambda: down().start(), finish_down)], [(start_up, finish_up)]

    def line_stage(self, job, start, size, last):
        n, i = self.n, self.dp
        shard = size // n
        per_side = n if last else n - 1
        base, place, y = self.take(2 * per_side, (2 * n + 1 if last else n + 1) * shard, 0 if last else 2)
        right = {"dp": jnp.minimum(i + 1, n - 1)}
        left = {"dp": jnp.maximum(i - 1, 0)}

        def part(j):
            return self.view(job, start + j * shard, shard)

        def op(s, going_up):
            k = base + 2 * (s + 1 if going_up and last and s == n - 2 else s)
            if going_up:
                send_r, send_l, take_r, take_l = i - s, i + s, i - 1 - s, i + 1 + s
                ok_sr, ok_sl = (i <= n - 2) & (send_r >= 0), (i >= 1) & (send_l <= n - 1)
                ok_tr, ok_tl = (i >= 1) & (take_r >= 0), (i <= n - 2) & (take_l <= n - 1)
            else:
                send_r, send_l, take_r, take_l = n - 1 - s + i, s + i - n + 1, n - 2 - s + i, s + i - n + 2
                ok_sr, ok_sl = (i <= n - 2) & (i <= s), (i >= 1) & (i >= n - 1 - s)
                ok_tr, ok_tl = (i >= 1) & (i - 1 <= s), (i <= n - 2) & (i >= n - 2 - s)

            def there(j, from_right):
                if going_up:
                    return self.landing(job, place + (n + 1 + j) * shard, shard) if last else part(j)
                slot = n if from_right and s == n - 2 else j
                return self.landing(job, place + slot * shard, shard)

            def to_right(j):
                return self.copy(job, k, part(j), there(j, False), right, 0)

            def to_left(j):
                return self.copy(job, k + 1, part(j), there(j, True), left, 1)

            def begin():
                if going_up and not last and s == 0:
                    pl.when(i >= 1)(lambda: pl.semaphore_wait(self.ack(job, y), 1))
                    pl.when(i <= n - 2)(lambda: pl.semaphore_wait(self.ack(job, y + 1), 1))
                pl.when(ok_sr)(lambda: to_right(send_r).start())
                pl.when(ok_sl)(lambda: to_left(send_l).start())

            def finish():
                def took(copy, j, slot):
                    copy.wait_recv()
                    if not going_up:
                        self.combine(job, start + j * shard, place + slot * shard, shard, True)
                    elif last:
                        self.combine(job, start + j * shard, place + (n + 1 + j) * shard, shard, False)

                pl.when(ok_tr)(lambda: took(to_right(take_r), take_r, take_r))
                pl.when(ok_tl)(lambda: took(to_left(take_l), take_l, n if s == n - 2 else take_l))
                pl.when(ok_sr)(lambda: to_right(send_r).wait_send())
                pl.when(ok_sl)(lambda: to_left(send_l).wait_send())
                if not going_up and not last and s == n - 2:
                    pl.when(i <= n - 2)(lambda: self.signal(job, y, right))
                    pl.when(i >= 1)(lambda: self.signal(job, y + 1, left))

            return begin, finish

        return start + i * shard, shard, [op(s, False) for s in range(n - 1)], [op(s, True) for s in range(n - 1)]

    def peer_block(self, o):
        return pltpu.make_async_remote_copy(
            self.G.at[BLOCKS + o % 2],
            self.peer_buf.at[o],
            self.peer_send.at[o],
            self.peer_recv.at[o],
            device_id={"section": 1 - self.sec},
            device_id_type=MESH,
        )

    def fetch(self, o):
        return pltpu.make_async_copy(self.peer_buf.at[o], self.ST, self.load.at[0])

    def result(self, o, remote):
        dst = self.outs.at[o % OWN * 2 + self.sec]
        if remote:
            return pltpu.make_async_remote_copy(
                self.G.at[o],
                dst,
                self.out.at[o],
                self.out_recv.at[o],
                device_id={"section": 1 - self.sec},
                device_id_type=MESH,
            )
        return pltpu.make_async_copy(self.G.at[o], dst, self.out.at[o])

    def output(self, o):
        layer = 1 - o // OWN
        pl.when(layer == self.sec)(lambda: self.result(o, False).start())
        pl.when(layer != self.sec)(lambda: self.result(o, True).start())

    def wait_output(self, o):
        layer = 1 - o // OWN

        @pl.when(layer == self.sec)
        def _():
            self.result(o, False).wait()
            self.result(o, True).wait_recv()

        @pl.when(layer != self.sec)
        def _():
            self.result(o, True).wait_send()

    def step(self, o, k):
        if k == 0:
            self.peer_block(o).wait_recv()
            self.fetch(o).start()
            return
        if k == 1:
            self.fetch(o).wait()

            def body(i, _):
                rows = pl.ds(pl.multiple_of(i % 8 * 96, 96), 96)
                third = i // 8
                self.G[o, third, rows, :] = self.G[o, third, rows, :] + self.ST[third, rows, :]
                return 0

            lax.fori_loop(0, 24, body, 0)

        def advance(kind, typ):
            ops = self.plan((o, typ), kind, typ)
            if k >= 2:
                ops[k - 2][1]()
            if k - 1 < len(ops):
                ops[k - 1][0]()

        advance(0, jnp.int32(0))

        def rest(typ, _):
            advance(1, typ)
            return 0

        lax.fori_loop(1, 3, rest, 0)
        if k == self.steps - 1:
            self.output(o)

    def slot(self, t):
        for k in reversed(range(self.steps)):
            times = [row[k] for row in self.table]
            words = []
            for w in range(times[-1] // 31 + 1):
                words.append(sum(1 << (time - 31 * w) for time in times if 0 <= time - 31 * w < 31))
            word = jnp.int32(words[-1])
            for w in reversed(range(len(words) - 1)):
                word = jnp.where(t < 31 * (w + 1), jnp.int32(words[w]), word)

            @pl.when(((word >> (t % 31)) & 1 == 1) & (t <= times[-1]))
            def _(k=k, times=times):
                o = jnp.int32(0)
                for time in times[:-1]:
                    o = o + jnp.where(t > time, 1, 0)
                self.step(o, k)


    @property
    def slots(self):
        return self.table[-1][-1] + 1


def backward_kernel(
    dp_size, rep_size,
    cot, segs, wall, xs, qkvs, lses, atts, n1s, nbs, us, n2s, rss, tabs, biases, smalls,
    blocks, grad_small, ing, peer_buf,
    G, RB, ST, WR, UP, N2, NB, DB, DJ, N1, ATT, QK, U, DAT, DN, TAB, BIAS, RS, LSE, SM, SG, SB, SP,
    wsem, lsem, usem, send, recv, load, out, out_recv, peer_send, peer_recv, gsem, ssend, srecv, sync,
):
    sec = lax.axis_index("section")
    dp = lax.axis_index("dp")
    rep = lax.axis_index("rep")
    peer = {"section": 1 - sec}
    tokens = UP.shape[0]
    sums = Blocks(
        G, RB, ST, peer_buf, blocks,
        (send, recv, load, out, out_recv, peer_recv, peer_send, sync), dp, rep, dp_size, rep_size,
    )

    def weight(seq):
        layer, b = 1 - seq // BLOCKS, seq % BLOCKS
        return pltpu.make_async_copy(wall.at[layer, b], WR.at[b % 4], wsem.at[b % 4])

    def u_copy(layer, f):
        return pltpu.make_async_copy(us.at[layer, f], U.at[f % 2], usem.at[f % 2])

    def loads(layer):
        return (
            pltpu.make_async_copy(n2s.at[layer], N2, lsem.at[0]),
            pltpu.make_async_copy(nbs.at[layer], NB, lsem.at[1]),
            pltpu.make_async_copy(n1s.at[layer], N1, lsem.at[2]),
            pltpu.make_async_copy(atts.at[layer], ATT, lsem.at[3]),
            pltpu.make_async_copy(qkvs.at[layer], QK, lsem.at[4]),
            pltpu.make_async_copy(rss.at[layer], RS, lsem.at[5]),
            pltpu.make_async_copy(lses.at[layer], LSE, lsem.at[6]),
            pltpu.make_async_copy(xs.at[layer], N2, lsem.at[7]),
        )

    first = (
        pltpu.make_async_copy(cot.at[sec], UP, lsem.at[8]),
        pltpu.make_async_copy(smalls, SM, lsem.at[9]),
        pltpu.make_async_copy(tabs, TAB, lsem.at[10]),
        pltpu.make_async_copy(biases, BIAS, lsem.at[11]),
    )
    for copy in first:
        copy.start()

    barrier = pltpu.get_barrier_semaphore()
    partners = [(peer, None)]
    partners += [({"rep": rep ^ (1 << b)}, None) for b in range(rep_size.bit_length() - 1)]
    partners += [({"dp": dp ^ (1 << b)}, None) for b in range(dp_size.bit_length() - 1)]
    if sums.line:
        partners += [({"dp": jnp.minimum(dp + 1, dp_size - 1)}, dp < dp_size - 1)]
        partners += [({"dp": jnp.maximum(dp - 1, 0)}, dp > 0)]
    count = 0
    for device, valid in partners:

        def greet(device=device):
            pl.semaphore_signal(barrier, inc=1, device_id=device, device_id_type=MESH)

        if valid is None:
            greet()
            count = count + 1
        else:
            pl.when(valid)(greet)
            count = count + jnp.where(valid, 1, 0)
    pl.semaphore_wait(barrier, count)

    for seq in range(4):
        weight(seq).start()
    real = jnp.where(own_segments(segs, sec)[1] < SLOT // MINLEN, 1.0, 0.0).astype(F32)

    def in_copies(layer):
        mine = pltpu.make_async_copy(UP, ing.at[sec], gsem.at[0])
        theirs = pltpu.make_async_remote_copy(
            UP, ing.at[sec], gsem.at[1], gsem.at[2], device_id=peer, device_id_type=MESH
        )
        return mine, theirs

    def layer_step(li, _):
        layer = 1 - li
        copies = loads(layer)
        for copy in copies[:7]:
            copy.start()
        u_copy(layer, 0).start()
        u_copy(layer, 1).start()

        def slot(s):
            sums.slot(li * CALLS + s)

        def outer(lhs, rhs, b):
            o = li * OWN + b // 2
            mine = b % 2 == sec

            @pl.when(~mine & (o >= 2))
            def _():
                sums.peer_block(o - 2).wait_send()

            t = jnp.where(mine, o, BLOCKS + o % 2)
            for c in range(3):
                cols = slice(c * 256, (c + 1) * 256)
                G[t, c] = dot_tn(lhs[...], rhs[:, cols]).astype(BF16)

            pl.when(~mine)(lambda: sums.peer_block(o).start())

        @pl.when(li == 0)
        def _():
            for copy in first:
                copy.wait()
            UP[...] = (UP[...].astype(F32) * real).astype(BF16)

        copies[0].wait()
        copies[5].wait()

        def norm_back(grad, n, gain, scale):
            a = grad * gain
            m1 = jnp.mean(a, axis=1, keepdims=True)
            m2 = jnp.mean(a * n, axis=1, keepdims=True)
            return (a - m1 - n * m2) * scale

        def rows_sum(value):
            return jnp.sum(value, axis=0, keepdims=True)

        for row in (G_FFN, B_FFN, B_DOWN, G_ATTN, B_ATTN, B_OUT):
            SG[layer, row] = jnp.zeros((1, D), F32)
        for row in (13, 14, 15):
            SG[layer, row] = jnp.zeros((1, D), F32)

        def second_norm(c, _):
            rows = pl.ds(pl.multiple_of(c * 256, 256), 256)
            up = UP[rows, :].astype(F32)
            n = N2[rows, :].astype(F32)
            scale = RS[1, rows, 0:1]
            g = norm_back(up, n, SM[layer, G_FFN], scale)
            DN[rows, :] = g
            DB[rows, :] = g.astype(BF16)
            SG[layer, G_FFN] += rows_sum(up * n)
            SG[layer, B_FFN] += rows_sum(up)
            SG[layer, B_DOWN] += rows_sum(g)
            return 0

        lax.fori_loop(0, tokens // 256, second_norm, 0)
        copies[7].start()
        copies[1].wait()

        def ffn(f, _):
            u_copy(layer, f).wait()
            weight(li * BLOCKS + 2 * f).wait()
            weight(li * BLOCKS + 2 * f + 1).wait()
            down, up = WR.at[2 * f % 4], WR.at[(2 * f + 1) % 4]
            for c in range(3):
                cols = slice(c * 256, (c + 1) * 256)
                u = U[f % 2, :, cols].astype(F32)
                square, t = gelu_parts(u)
                lift = 1.0 + t
                DJ[1, :, cols] = (0.5 * u * lift).astype(BF16)
                slope = 0.5 * lift * (1.0 + u * (1.0 - t) * (GELU_A * (1.0 + 3.0 * GELU_B * square)))
                grad = dot_t(DB[...], down[cols, :]) * slope
                SG[layer, B_IN + f, :, cols] = rows_sum(grad)
                DJ[0, :, cols] = grad.astype(BF16)
            outer(DJ.at[1], DB, 2 * f)
            slot(2 * f)
            outer(NB, DJ.at[0], 2 * f + 1)
            for c in range(3):
                cols = slice(c * 256, (c + 1) * 256)
                DN[:, cols] += dot_t(DJ[0], up[cols, :])
            weight(li * BLOCKS + 2 * f + 4).start()
            weight(li * BLOCKS + 2 * f + 5).start()
            pl.when(f + 2 < CHUNKS)(lambda: u_copy(layer, f + 2).start())
            slot(2 * f + 1)
            return 0

        lax.fori_loop(0, CHUNKS, ffn, 0)
        copies[2].wait()

        def first_norm(c, _):
            rows = pl.ds(pl.multiple_of(c * 256, 256), 256)
            up = DN[rows, :]
            n = N1[rows, :].astype(F32)
            g = norm_back(up, n, SM[layer, G_ATTN], RS[0, rows, 0:1])
            DN[rows, :] = g
            DB[rows, :] = g.astype(BF16)
            SG[layer, G_ATTN] += rows_sum(up * n)
            SG[layer, B_ATTN] += rows_sum(up)
            SG[layer, B_OUT] += rows_sum(g)
            return 0

        lax.fori_loop(0, tokens // 256, first_norm, 0)
        copies[3].wait()
        outer(ATT, DB, OUT)
        weight(li * BLOCKS + OUT).wait()
        w_out = WR.at[OUT % 4]
        for c in range(3):
            cols = slice(c * 256, (c + 1) * 256)
            DAT[:, cols] = dot_t(DB[...], w_out[cols, :]).astype(BF16)
        pl.when(li == 0)(lambda: weight(BLOCKS).start())
        slot(2 * CHUNKS)
        copies[4].wait()
        copies[6].wait()

        def pair(hp, _):
            lanes = pl.ds(pl.multiple_of(hp * 128, 128), 128)
            q2 = QK[0, :, lanes]
            k2 = QK[1, :, lanes]
            v2 = QK[2, :, lanes]
            o2 = DAT[:, lanes]
            low = low_lanes(k2.shape)
            k_t = k2.T
            zero = jnp.zeros_like(k2)
            grads_q, grads_k, grads_v = [], [], []
            for h in range(2):
                mask = low if h == 0 else ~low
                s = dot_t(jnp.where(mask, k2, zero), q2) * SCORE + BIAS[...]
                p = jnp.exp2(s - LSE[hp, h : h + 1, :])
                dprob = dot_t(jnp.where(mask, v2, zero), o2)
                inner = jnp.sum(p * dprob, axis=0, keepdims=True)
                ds = (p * (dprob - inner)).astype(BF16)
                grads_v.append(dot(p.astype(BF16), o2))
                grads_k.append(dot(ds, q2))
                grads_q.append(dot(k_t[h * HEAD : (h + 1) * HEAD], ds))
            scale = 1.0 / math.sqrt(HEAD)
            gq = jnp.concatenate(grads_q, axis=0).T * scale
            gk = jnp.where(low, grads_k[0], grads_k[1]) * scale
            gv = jnp.where(low, grads_v[0], grads_v[1])
            cos, sin = TAB[0], TAB[1]
            gq = gq * cos - swap_halves(gq) * sin
            gk = gk * cos - swap_halves(gk) * sin
            for third, g in enumerate((gq, gk, gv)):
                DJ[third, :, lanes] = g.astype(BF16)
                SG[layer, B_QKV + third, :, lanes] = rows_sum(g)
            slot(2 * CHUNKS + 1 + hp)
            return 0

        lax.fori_loop(0, PAIRS, pair, 0)
        copies[7].wait()

        def third_step(third, _):
            outer(N2, DJ.at[third], QKV + third)
            weight(li * BLOCKS + QKV + third).wait()
            w = WR.at[(QKV + third) % 4]
            for c in range(3):
                cols = slice(c * 256, (c + 1) * 256)
                DN[:, cols] += dot_t(DJ[third], w[cols, :])
            pl.when(li == 0)(lambda: weight(BLOCKS + 1 + third).start())
            slot(CALLS - 3 + third)
            return 0

        lax.fori_loop(0, 3, third_step, 0)

        mine, theirs = in_copies(layer)
        @pl.when(li == 1)
        def _():
            pl.when(sec == 1)(lambda: mine.wait())
            pl.when(sec == 0)(lambda: theirs.wait_send())

        UP[...] = DN[...].astype(BF16)
        pl.when(layer == sec)(lambda: mine.start())
        pl.when(layer != sec)(lambda: theirs.start())
        return 0

    lax.fori_loop(0, 2, layer_step, 0)

    small_partners = [peer] + [device for device, valid in partners[1:] if valid is None]

    def small_copy(m):
        src = SG.at[1 - sec] if m == 0 else SP.at[m - 1]
        return pltpu.make_async_remote_copy(
            src, SB.at[m], ssend.at[m], srecv.at[m], device_id=small_partners[m], device_id_type=MESH
        )

    small_copy(0).start()

    def small_step(m):
        small_copy(m).wait_recv()
        SP[m] = (SG[sec] if m == 0 else SP[m - 1]) + SB[m]
        if m + 1 < len(small_partners):
            small_copy(m + 1).start()

    rounds = max(sums.slots - 2 * CALLS, len(small_partners))

    def final(i, _):
        sums.slot(2 * CALLS + i)
        for m in range(len(small_partners)):
            pl.when(i == m)(functools.partial(small_step, m))
        return 0

    lax.fori_loop(0, rounds, final, 0)
    for m in range(len(small_partners)):
        small_copy(m).wait_send()
    small_out = pltpu.make_async_copy(SP.at[len(small_partners) - 1], grad_small, ssend.at[0])
    small_out.start()

    for o in (BLOCKS - 2, BLOCKS - 1):
        sums.peer_block(o).wait_send()

    def out_wait(o, _):
        sums.wait_output(o)
        return 0

    lax.fori_loop(0, BLOCKS, out_wait, 0)
    small_out.wait()
    mine, theirs = in_copies(0)
    pl.when(sec == 0)(lambda: mine.wait())
    pl.when(sec == 1)(lambda: theirs.wait_send())
    theirs.wait_recv()


RING = 6


def convert_kernel(
    blocks, small,
    out_q, out_o, out_i, out_d, b_q, b_o, g_a, b_a, b_i, b_d, g_f, b_f,
    LOW, HIGH, isem, osem,
):
    tiles = []
    for b in range(BLOCKS):
        for c in range(3):
            cols = pl.ds(c * THIRD, THIRD)
            if b < OUT and b % 2 == 0:
                dst = out_d.at[0, pl.ds(b // 2 * D, D), cols]
            elif b < OUT:
                dst = out_i.at[0, :, pl.ds(b // 2 * D + c * THIRD, THIRD)]
            elif b == OUT:
                dst = out_o.at[0, :, cols]
            else:
                dst = out_q.at[0, :, pl.ds((b - QKV) * D + c * THIRD, THIRD)]
            tiles.append((blocks.at[b, c], dst))
    reads = [pltpu.make_async_copy(src, LOW.at[i % RING], isem.at[i % RING]) for i, (src, _) in enumerate(tiles)]
    writes = [pltpu.make_async_copy(HIGH.at[i % RING], dst, osem.at[i % RING]) for i, (_, dst) in enumerate(tiles)]
    for i in range(RING):
        reads[i].start()
    for row, ref in ((B_QKV, b_q), (B_OUT, b_o), (G_ATTN, g_a), (B_ATTN, b_a), (B_IN, b_i), (B_DOWN, b_d), (G_FFN, g_f), (B_FFN, b_f)):
        for i in range(ref.shape[1] // D):
            ref[0:1, i * D : (i + 1) * D] = small[row + i]
    for i in range(len(tiles)):
        reads[i].wait()
        if i >= RING:
            writes[i - RING].wait()

        def body(r, _, at=i % RING):
            rows = pl.ds(pl.multiple_of(r * 192, 64), 192)
            HIGH[at, rows, :] = LOW[at, rows, :].astype(F32)
            return 0

        lax.fori_loop(0, 4, body, 0)
        writes[i].start()
        if i + RING < len(tiles):
            reads[i + RING].start()
    for write in writes[len(tiles) - RING :]:
        write.wait()


def per_device(
    dp_size, rep_size, inputs, segments, cotangent, w_qkv, b_qkv, w_out, b_out, g_attn, b_attn, w_in, b_in, w_down,
    b_down, g_ffn, b_ffn,
):
    tokens = inputs.shape[1]
    anywhere = pl.BlockSpec(memory_space=pl.ANY)
    in_vmem = pl.BlockSpec(memory_space=pltpu.VMEM)

    def shape(*dims, dtype=BF16):
        return jax.ShapeDtypeStruct(dims, dtype)

    def mem(*dims, dtype=BF16):
        return pltpu.VMEM(dims, dtype)

    dma = pltpu.SemaphoreType.DMA
    stash = pl.pallas_call(
        forward_kernel,
        out_shape=(
            shape(2, BLOCKS, D, D),
            shape(2, tokens, D),
            shape(2, 3, tokens, D),
            shape(2, PAIRS, 8, tokens, dtype=F32),
            shape(2, tokens, D),
            shape(2, tokens, D),
            shape(2, tokens, D),
            shape(2, CHUNKS, tokens, D),
            shape(2, tokens, D),
            shape(2, 2, tokens, 128, dtype=F32),
            shape(2, tokens, 128, dtype=F32),
            shape(tokens, tokens, dtype=F32),
            shape(2, tokens, D),
            shape(2, SMALL, 1, D, dtype=F32),
        ),
        in_specs=[anywhere, in_vmem] + [anywhere] * 4 + [in_vmem] * 8,
        out_specs=(anywhere,) * 14,
        scratch_shapes=[
            mem(2, BLOCKS, D, D),
            mem(2, SMALL, 1, D, dtype=F32),
            mem(3, tokens, D),
            mem(2, 3, tokens, D),
            mem(2, PAIRS, 8, tokens, dtype=F32),
            mem(2, tokens, D),
            mem(2, tokens, D),
            mem(2, tokens, D),
            mem(2, CHUNKS, tokens, D),
            mem(2, tokens, D),
            mem(2, 2, tokens, 128, dtype=F32),
            mem(2, tokens, 128, dtype=F32),
            mem(tokens, tokens, dtype=F32),
            mem(tokens, D, dtype=F32),
            mem(tokens, D),
            dma((BLOCKS,)),
            dma((BLOCKS,)),
            dma((BLOCKS,)),
            dma((6,)),
            dma((2, BLOCKS)),
            dma((2, 9)),
            dma((3,)),
        ],
        compiler_params=pltpu.CompilerParams(collective_id=0, has_side_effects=True, vmem_limit_bytes=VMEM_LIMIT),
        name="forward",
    )(inputs, segments, w_qkv, w_out, w_in, w_down, b_qkv, b_out, g_attn, b_attn, b_in, b_down, g_ffn, b_ffn)
    (wall, xs, qkvs, lses, atts, n1s, nbs, us, n2s, rss, tabs, biases, acts, smalls) = stash

    line = dp_size == 4 and rep_size == 4
    bits = dp_size.bit_length() + rep_size.bit_length() - 2
    ring = BLOCKS
    landing = 1152 if line else 912
    out = pl.pallas_call(
        functools.partial(backward_kernel, dp_size, rep_size),
        out_shape=(
            shape(BLOCKS, 3, D, THIRD),
            shape(SMALL, 1, D, dtype=F32),
            shape(2, tokens, D),
            shape(BLOCKS, 3, D, THIRD),
        ),
        in_specs=[anywhere, in_vmem] + [anywhere] * 13,
        out_specs=(anywhere,) * 4,
        scratch_shapes=[
            mem(BLOCKS + 2, 3, D, THIRD),
            mem(ring, 3, landing, THIRD),
            mem(3, D, THIRD),
            mem(4, D, D),
            mem(tokens, D),
            mem(tokens, D),
            mem(tokens, D),
            mem(tokens, D),
            mem(3, tokens, D),
            mem(tokens, D),
            mem(tokens, D),
            mem(3, tokens, D),
            mem(2, tokens, D),
            mem(tokens, D),
            mem(tokens, D, dtype=F32),
            mem(2, tokens, 128, dtype=F32),
            mem(tokens, tokens, dtype=F32),
            mem(2, tokens, 128, dtype=F32),
            mem(PAIRS, 8, tokens, dtype=F32),
            mem(2, SMALL, 1, D, dtype=F32),
            mem(2, SMALL, 1, D, dtype=F32),
            mem(bits + 1, SMALL, 1, D, dtype=F32),
            mem(bits + 1, SMALL, 1, D, dtype=F32),
            dma((4,)),
            dma((12,)),
            dma((2,)),
            dma((3 * ring, 2)),
            dma((3 * ring, 10)),
            dma((1,)),
            dma((BLOCKS,)),
            dma((BLOCKS,)),
            dma((BLOCKS,)),
            dma((BLOCKS,)),
            dma((3,)),
            dma((bits + 1,)),
            dma((bits + 1,)),
            pltpu.SemaphoreType.REGULAR((3 * ring, 3)),
        ],
        compiler_params=pltpu.CompilerParams(collective_id=1, has_side_effects=True, vmem_limit_bytes=VMEM_LIMIT),
        name="backward",
    )(cotangent, segments, wall, xs, qkvs, lses, atts, n1s, nbs, us, n2s, rss, tabs, biases, smalls)
    blocks, grad_small, ing, _ = out
    vectors = (3 * D, D, D, D, CHUNKS * D, D, D, D)
    grads = pl.pallas_call(
        convert_kernel,
        out_shape=(
            *(shape(1, *dims, dtype=F32) for dims in ((D, 3 * D), (D, D), (D, CHUNKS * D), (CHUNKS * D, D))),
            *(shape(1, size, dtype=F32) for size in vectors),
        ),
        in_specs=[anywhere, in_vmem],
        out_specs=(anywhere,) * 4 + (in_vmem,) * 8,
        scratch_shapes=[
            mem(RING, D, THIRD),
            mem(RING, D, THIRD, dtype=F32),
            dma((RING,)),
            dma((RING,)),
        ],
        compiler_params=pltpu.CompilerParams(vmem_limit_bytes=VMEM_LIMIT),
        name="convert",
    )(blocks, grad_small)
    grad_q, grad_o, grad_i, grad_d, b_q, b_o, g_a, b_a, b_i, b_d, g_f, b_f = grads
    return acts[None], ing[None], grad_q, b_q, grad_o, b_o, g_a, b_a, grad_i, b_i, grad_d, b_d, g_f, b_f


def solution(mesh):
    tokens = ("dp", "rep")
    weight, vector = P("section", None, None), P("section", None)
    weights = (weight, vector, weight, vector, vector, vector, weight, vector, weight, vector, vector, vector)
    activations = P("section", None, tokens, None)
    return jax.shard_map(
        functools.partial(per_device, mesh.shape["dp"], mesh.shape["rep"]),
        mesh=mesh,
        in_specs=(P(None, tokens, None), P(None, tokens), P(None, tokens, None), *weights),
        out_specs=(activations, activations, *weights),
        check_vma=False,
    )
```

```python
import functools
import math

import jax
import jax.numpy as jnp
from jax import lax
from jax.experimental import pallas as pl
from jax.experimental.pallas import tpu as pltpu
from jax.sharding import PartitionSpec as P

D = 768
HEADS = 12
HEAD = 64
PAIRS = HEADS // 2
SLOT = 512
MINLEN = 64
CHUNKS = 4
OUT = 2 * CHUNKS
QKV = OUT + 1
BLOCKS = QKV + 3
SEND_ORDER = (9, 10, 11, 8, 1, 0, 3, 2, 5, 4, 7, 6)
B_QKV, B_OUT, G_ATTN, B_ATTN, B_IN, B_DOWN, G_FFN, B_FFN = 0, 3, 4, 5, 6, 10, 11, 12
SMALL = 16
EPSILON = 1e-05
NEG_LARGE = -1e30
LOG2E = math.log2(math.e)
SCORE = LOG2E / math.sqrt(HEAD)
GELU_A = math.sqrt(2.0 / math.pi)
GELU_B = 0.044715
THIRD = D // 3
OWN = BLOCKS // 2
CALLS = 18
FINAL = 2 * CALLS
TABLE = (
    (1, 2, 5, 8, 11, 14, 16, 18, 21, 24, 27, 30),
    (3, 4, 7, 10, 13, 16, 18, 20, 23, 26, 29, 32),
    (5, 6, 9, 12, 15, 18, 20, 22, 25, 28, 31, 34),
    (7, 8, 11, 14, 17, 20, 22, 24, 27, 30, 33, 36),
    (15, 16, 19, 22, 25, 28, 30, 32, 35, 36, 37, 38),
    (17, 18, 21, 24, 27, 30, 32, 34, 36, 37, 38, 39),
    (19, 20, 23, 26, 29, 32, 34, 36, 37, 38, 39, 40),
    (21, 22, 25, 28, 31, 34, 36, 37, 38, 39, 40, 41),
    (23, 24, 27, 30, 33, 36, 37, 38, 39, 40, 41, 42),
    (25, 26, 29, 32, 35, 37, 38, 39, 40, 41, 42, 43),
    (33, 34, 36, 37, 38, 39, 40, 41, 42, 43, 44, 45),
    (35, 36, 37, 38, 39, 40, 41, 42, 43, 44, 45, 46),
)


def timetable(steps):
    ready = [CALLS * li + at for li in range(2) for at in (1, 3, 5, 7, 15, 17)]
    table = []
    for o, first in enumerate(ready):
        times = []
        for k in range(steps):
            t = max(first, times[-1] + 1 if k else 0, table[-1][k] + 1 if o else 0)
            times.append(t)
        table.append(times)
    return table


MESH = pl.DeviceIdType.MESH
F32 = jnp.float32
BF16 = jnp.bfloat16
VMEM_LIMIT = 62 * 1024 * 1024


def dot(a, b):
    return lax.dot_general(a, b, (((1,), (0,)), ((), ())), preferred_element_type=F32)


def dot_t(a, b):
    return lax.dot_general(a, b, (((1,), (1,)), ((), ())), preferred_element_type=F32)


def dot_tn(a, b):
    return lax.dot_general(a, b, (((0,), (0,)), ((), ())), preferred_element_type=F32)


def swap_halves(t):
    lane = lax.broadcasted_iota(jnp.int32, t.shape, 1)
    return jnp.where(lane % HEAD < HEAD // 2, pltpu.roll(t, 96, 1), pltpu.roll(t, 32, 1))


def low_lanes(shape):
    return lax.broadcasted_iota(jnp.int32, shape, 1) < HEAD


def own_segments(segs, sec):
    row = jnp.where(sec == 0, segs[0:1, :], segs[1:2, :]).astype(F32)
    return row, jnp.broadcast_to(row, (128, row.shape[1])).T[:, 0:1]


def gelu_parts(u):
    square = u * u
    t = jnp.tanh(GELU_A * u * (1.0 + GELU_B * square))
    return square, t


def forward_kernel(
    inp, segs, wq, wo, wi, wd, bq, bo, ga, ba, bi, bd, gf, bf,
    wall, xs, qkvs, lses, atts, n1s, nbs, us, n2s, rss, tabs, biases, acts, smalls,
    W, SM, X, QK, LSE, ATT, N1, NB, U, N2, RS, TAB, BIAS, ACC, ACT,
    osem, rsend, rrecv, ssem, wsem, stash, asem,
):
    sec = lax.axis_index("section")
    other = 1 - sec
    peer = {"section": other}
    tokens = X.shape[1]

    def source(b):
        if b < OUT:
            part = pl.ds(b // 2 * D, D)
            return wd.at[0, part, :] if b % 2 == 0 else wi.at[0, :, part]
        if b == OUT:
            return wo.at[0]
        return wq.at[0, :, pl.ds((b - QKV) * D, D)]

    def own_copy(b):
        return pltpu.make_async_copy(source(b), W.at[sec, b], osem.at[b])

    def peer_copy(b):
        return pltpu.make_async_remote_copy(
            source(b), W.at[sec, b], rsend.at[b], rrecv.at[b], device_id=peer, device_id_type=MESH
        )

    load_x = pltpu.make_async_copy(inp.at[sec], X.at[0], ssem.at[0])
    load_x.start()
    for b in SEND_ORDER[:4]:
        own_copy(b).start()
    barrier = pltpu.get_barrier_semaphore()
    pl.semaphore_signal(barrier, inc=1, device_id=peer, device_id_type=MESH)
    pl.semaphore_wait(barrier, 1)
    for row, ref in ((B_QKV, bq), (B_OUT, bo), (G_ATTN, ga), (B_ATTN, ba), (B_IN, bi), (B_DOWN, bd), (G_FFN, gf), (B_FFN, bf)):
        for i in range(ref.shape[1] // D):
            SM[sec, row + i] = ref[0:1, i * D : (i + 1) * D].astype(F32)
    for row in range(B_FFN + 1, SMALL):
        SM[sec, row] = jnp.zeros((1, D), F32)
    small_copy = pltpu.make_async_remote_copy(
        SM.at[sec], SM.at[sec], ssem.at[1], ssem.at[2], device_id=peer, device_id_type=MESH
    )
    small_copy.start()
    for b in SEND_ORDER:
        peer_copy(b).start()
    for b in SEND_ORDER[4:]:
        own_copy(b).start()

    row_at = lax.broadcasted_iota(jnp.int32, (tokens, tokens), 0)
    col_at = lax.broadcasted_iota(jnp.int32, (tokens, tokens), 1)
    seg_row, seg_col = own_segments(segs, sec)
    same = seg_col == seg_row
    position = jnp.sum(jnp.where(same & (col_at < row_at), 1.0, 0.0), axis=1, keepdims=True)
    allowed = (same & (seg_col < SLOT // MINLEN)) | (row_at == col_at)
    BIAS[...] = jnp.where(allowed, 0.0, NEG_LARGE)
    lane = lax.broadcasted_iota(jnp.int32, (1, 128), 1)
    frequency = jnp.exp((lane % 32).astype(F32) * (-2.0 * math.log(10000.0) / HEAD))
    angle = position * frequency
    TAB[0] = jnp.cos(angle)
    sine = jnp.sin(angle)
    TAB[1] = jnp.where(lane % HEAD < HEAD // 2, -sine, sine)
    table_out = pltpu.make_async_copy(TAB, tabs, ssem.at[3])
    table_out.start()
    bias_out = pltpu.make_async_copy(BIAS, biases, ssem.at[4])
    bias_out.start()
    load_x.wait()
    small_copy.wait()
    small_out = pltpu.make_async_copy(SM, smalls, ssem.at[5])
    small_out.start()

    def keep(k, layer, src, dst):
        pltpu.make_async_copy(src.at[layer], dst.at[layer], stash.at[layer, k]).start()

    def layer_step(layer, _):
        def ready(b):
            @pl.when(layer == sec)
            def _():
                pltpu.make_async_copy(wo.at[0], W.at[sec, b], osem.at[b]).wait()

            @pl.when(layer != sec)
            def _():
                pltpu.make_async_remote_copy(
                    wo.at[0], W.at[other, b], rsend.at[b], rrecv.at[b], device_id=peer, device_id_type=MESH
                ).wait_recv()

            pltpu.make_async_copy(W.at[layer, b], wall.at[layer, b], wsem.at[layer, b]).start()

        keep(0, layer, X, xs)
        for third in range(3):
            ready(QKV + third)

            for c in range(3):
                cols = slice(c * 256, (c + 1) * 256)
                joined = dot(X[layer], W[layer, QKV + third, :, cols]) + SM[layer, B_QKV + third, :, cols]
                if third == 2:
                    QK[layer, third, :, cols] = joined.astype(BF16)
                else:
                    parts = []
                    for h in range(2):
                        t = joined[:, h * 128 : (h + 1) * 128]
                        parts.append((t * TAB[0] + swap_halves(t) * TAB[1]).astype(BF16))
                    QK[layer, third, :, cols] = jnp.concatenate(parts, axis=1)
        keep(1, layer, QK, qkvs)

        def pair(hp, _):
            lanes = pl.ds(pl.multiple_of(hp * 128, 128), 128)
            q2 = QK[layer, 0, :, lanes]
            k2 = QK[layer, 1, :, lanes]
            v_t = QK[layer, 2, :, lanes].T
            low = low_lanes(k2.shape)
            outs = []
            for h in range(2):
                k_one = jnp.where(low if h == 0 else ~low, k2, jnp.zeros_like(k2))
                s = dot_t(k_one, q2) * SCORE + BIAS[...]
                peak = jnp.max(s, axis=0, keepdims=True)
                p = jnp.exp2(s - peak)
                total = jnp.sum(p, axis=0, keepdims=True)
                LSE[layer, hp, h : h + 1, :] = peak + jnp.log(total) * LOG2E
                outs.append(dot(v_t[h * HEAD : (h + 1) * HEAD], p.astype(BF16)) * (1.0 / total))
            ATT[layer, :, lanes] = jnp.concatenate(outs, axis=0).T.astype(BF16)
            return 0

        lax.fori_loop(0, PAIRS, pair, 0, unroll=6)
        keep(2, layer, LSE, lses)
        keep(3, layer, ATT, atts)
        ready(OUT)

        def norm_rows(r):
            mean = jnp.mean(r, axis=1, keepdims=True)
            centered = r - mean
            scale = lax.rsqrt(jnp.mean(centered * centered, axis=1, keepdims=True) + EPSILON)
            return centered * scale, scale

        def first_norm(c, _):
            rows = pl.ds(pl.multiple_of(c * 256, 256), 256)
            r = X[layer, rows, :].astype(F32) + dot(ATT[layer, rows, :], W[layer, OUT]) + SM[layer, B_OUT]
            n, scale = norm_rows(r)
            N1[layer, rows, :] = n.astype(BF16)
            RS[layer, 0, rows, :] = jnp.broadcast_to(scale, (256, 128))
            y = n * SM[layer, G_ATTN] + SM[layer, B_ATTN]
            NB[layer, rows, :] = y.astype(BF16)
            ACC[rows, :] = y + SM[layer, B_DOWN]
            return 0

        lax.fori_loop(0, tokens // 256, first_norm, 0, unroll=2)
        keep(4, layer, N1, n1s)
        keep(5, layer, NB, nbs)

        def ffn(f, _):
            ready(2 * f + 1)

            for c in range(3):
                cols = slice(c * 256, (c + 1) * 256)
                u = dot(NB[layer], W[layer, 2 * f + 1, :, cols]) + SM[layer, B_IN + f, :, cols]
                U[layer, f, :, cols] = u.astype(BF16)
                ACT[:, cols] = (0.5 * u * (1.0 + gelu_parts(u)[1])).astype(BF16)
            ready(2 * f)
            for c in range(3):
                cols = slice(c * 256, (c + 1) * 256)
                ACC[:, cols] += dot(ACT[...], W[layer, 2 * f, :, cols])
            return 0

        lax.fori_loop(0, CHUNKS, ffn, 0, unroll=2)
        keep(6, layer, U, us)

        def second_norm(c, _):
            rows = pl.ds(pl.multiple_of(c * 256, 256), 256)
            n, scale = norm_rows(ACC[rows, :])
            N2[layer, rows, :] = n.astype(BF16)
            RS[layer, 1, rows, :] = jnp.broadcast_to(scale, (256, 128))
            X[layer + 1, rows, :] = (n * SM[layer, G_FFN] + SM[layer, B_FFN]).astype(BF16)
            return 0

        lax.fori_loop(0, tokens // 256, second_norm, 0, unroll=2)
        keep(7, layer, N2, n2s)
        keep(8, layer, RS, rss)

        @pl.when(layer == sec)
        def _():
            pltpu.make_async_copy(X.at[layer + 1], acts.at[sec], asem.at[0]).start()

        @pl.when(layer != sec)
        def _():
            pltpu.make_async_remote_copy(
                X.at[layer + 1], acts.at[sec], asem.at[1], asem.at[2], device_id=peer, device_id_type=MESH
            ).start()

        return 0

    lax.fori_loop(0, 2, layer_step, 0)

    table_out.wait()
    bias_out.wait()
    small_out.wait()

    def finish(layer, _):
        for k, (src, dst) in enumerate(
            ((X, xs), (QK, qkvs), (LSE, lses), (ATT, atts), (N1, n1s), (NB, nbs), (U, us), (N2, n2s), (RS, rss))
        ):
            pltpu.make_async_copy(src.at[layer], dst.at[layer], stash.at[layer, k]).wait()
        for b in range(BLOCKS):
            pltpu.make_async_copy(W.at[layer, b], wall.at[layer, b], wsem.at[layer, b]).wait()
        return 0

    lax.fori_loop(0, 2, finish, 0)
    for b in range(BLOCKS):
        peer_copy(b).wait_send()
    pltpu.make_async_copy(X.at[1], acts.at[sec], asem.at[0]).wait()
    last = pltpu.make_async_remote_copy(
        X.at[1], acts.at[sec], asem.at[1], asem.at[2], device_id=peer, device_id_type=MESH
    )
    last.wait_send()
    last.wait_recv()


class Blocks:
    def __init__(self, G, RB, ST, peer_buf, outs, sems, dp, rep, dp_size, rep_size):
        self.G, self.RB, self.ST, self.peer_buf, self.outs = G, RB, ST, peer_buf, outs
        (self.send, self.recv, self.load, self.out, self.out_recv, self.peer_recv, self.peer_send, self.sync) = sems
        self.sec, self.dp, self.rep, self.n, self.rep_size = lax.axis_index("section"), dp, rep, dp_size, rep_size
        self.line = dp_size == 4 and rep_size == 4
        self.ring = RB.shape[0]
        for kind in (0, 1):
            self.steps = len(self.plan(jnp.int32(0), kind, jnp.int32(kind))) + 2
        self.table = TABLE if self.steps == len(TABLE[0]) else timetable(self.steps)

    def view(self, job, start, size):
        block, typ = job
        return self.G.at[block, typ, pl.ds(pl.multiple_of(start, 16), size), :]

    def landing(self, job, start, size):
        block, typ = job
        return self.RB.at[block % self.ring, typ, pl.ds(pl.multiple_of(start, 16), size), :]

    def copy(self, job, k, src, dst, device, side=0):
        block, typ = job
        slot = block % self.ring * 3 + typ
        return pltpu.make_async_remote_copy(
            src, dst, self.send.at[slot, side], self.recv.at[slot, k], device_id=device, device_id_type=MESH
        )

    def combine(self, job, start, place, size, add):
        step = next(n for n in (192, 96, 48) if size % n == 0)
        g = self.view(job, start, size)
        r = self.landing(job, place, size)

        def body(i, _):
            rows = pl.ds(pl.multiple_of(i * step, 16), step)
            g[rows, :] = g[rows, :] + r[rows, :] if add else r[rows, :]
            return 0

        lax.fori_loop(0, size // step, body, 0)

    def plan(self, job, kind, typ):
        if not isinstance(job, tuple):
            job = (job, typ)
        self.sem_at = 0
        self.sync_at = 0
        self.place_at = 0
        if self.line:
            bits = [("rep", typ - 1), ("rep", 2 - typ)] if kind else [("rep", job[0] & 1), ("rep", 1 - (job[0] & 1))]
            stages = bits + ["line"] if kind else ["line"] + bits
        else:
            stages = [("rep", b) for b in range(self.rep_size.bit_length() - 1)]
            stages += [("dp", b) for b in range(self.n.bit_length() - 1)]
        total, size = 0, D
        for stage in stages:
            if stage == "line":
                size //= self.n
                total += 1
            elif self.halves(size):
                size //= 2
                total += 1
        start, size, cuts = jnp.int32(0), D, 0
        down, up = [], []
        for stage in stages:
            if stage == "line":
                cuts += 1
                start, size, a, b = self.line_stage(job, start, size, cuts == total)
            elif self.halves(size):
                cuts += 1
                start, size, a, b = self.pair_stage(job, start, size, *stage, cuts == total)
            else:
                a, b = self.swap_stage(job, start, size, *stage), []
            down = down + a
            up = b + up
        assert self.sem_at <= self.recv.shape[1] and self.place_at <= self.RB.shape[2]
        assert self.sync_at <= self.sync.shape[1]
        return down + up

    @staticmethod
    def halves(size):
        return size // 2 % 48 == 0

    def take(self, sems, rows, syncs=0):
        k, place, y = self.sem_at, self.place_at, self.sync_at
        self.sem_at += sems
        self.place_at += rows
        self.sync_at += syncs
        return k, place, y

    def ack(self, job, y):
        return self.sync.at[job[0] % self.ring * 3 + job[1], y]

    def signal(self, job, y, device):
        pl.semaphore_signal(self.ack(job, y), inc=1, device_id=device, device_id_type=MESH)

    def swap_stage(self, job, start, size, axis, bit):
        index = self.rep if axis == "rep" else self.dp
        device = {axis: index ^ (1 << bit)}
        k, place, _ = self.take(1, size)

        def swap():
            return self.copy(job, k, self.view(job, start, size), self.landing(job, place, size), device)

        def finish():
            swap().wait()
            self.combine(job, start, place, size, True)

        return [(lambda: swap().start(), finish)]

    def pair_stage(self, job, start, size, axis, bit, last):
        index = self.rep if axis == "rep" else self.dp
        mine = (index >> bit) & 1
        device = {axis: index ^ (1 << bit)}
        half = size // 2
        kept, given = start + mine * half, start + (1 - mine) * half
        k, place, y = self.take(2 if last else 1, 2 * half if last else half, 0 if last else 1)

        def down():
            return self.copy(job, k, self.view(job, given, half), self.landing(job, place, half), device)

        def up():
            there = self.landing(job, place + half, half) if last else self.view(job, kept, half)
            return self.copy(job, k + 1 if last else k, self.view(job, kept, half), there, device)

        def finish_down():
            down().wait_recv()
            self.combine(job, kept, place, half, True)
            down().wait_send()
            if not last:
                self.signal(job, y, device)

        def start_up():
            if not last:
                pl.semaphore_wait(self.ack(job, y), 1)
            up().start()

        def finish_up():
            up().wait()
            if last:
                self.combine(job, given, place + half, half, False)

        return kept, half, [(lambda: down().start(), finish_down)], [(start_up, finish_up)]

    def line_stage(self, job, start, size, last):
        n, i = self.n, self.dp
        shard = size // n
        per_side = n if last else n - 1
        base, place, y = self.take(2 * per_side, (2 * n + 1 if last else n + 1) * shard, 0 if last else 2)
        right = {"dp": jnp.minimum(i + 1, n - 1)}
        left = {"dp": jnp.maximum(i - 1, 0)}

        def part(j):
            return self.view(job, start + j * shard, shard)

        def op(s, going_up):
            k = base + 2 * (s + 1 if going_up and last and s == n - 2 else s)
            if going_up:
                send_r, send_l, take_r, take_l = i - s, i + s, i - 1 - s, i + 1 + s
                ok_sr, ok_sl = (i <= n - 2) & (send_r >= 0), (i >= 1) & (send_l <= n - 1)
                ok_tr, ok_tl = (i >= 1) & (take_r >= 0), (i <= n - 2) & (take_l <= n - 1)
            else:
                send_r, send_l, take_r, take_l = n - 1 - s + i, s + i - n + 1, n - 2 - s + i, s + i - n + 2
                ok_sr, ok_sl = (i <= n - 2) & (i <= s), (i >= 1) & (i >= n - 1 - s)
                ok_tr, ok_tl = (i >= 1) & (i - 1 <= s), (i <= n - 2) & (i >= n - 2 - s)

            def there(j, from_right):
                if going_up:
                    return self.landing(job, place + (n + 1 + j) * shard, shard) if last else part(j)
                slot = n if from_right and s == n - 2 else j
                return self.landing(job, place + slot * shard, shard)

            def to_right(j):
                return self.copy(job, k, part(j), there(j, False), right, 0)

            def to_left(j):
                return self.copy(job, k + 1, part(j), there(j, True), left, 1)

            def begin():
                if going_up and not last and s == 0:
                    pl.when(i >= 1)(lambda: pl.semaphore_wait(self.ack(job, y), 1))
                    pl.when(i <= n - 2)(lambda: pl.semaphore_wait(self.ack(job, y + 1), 1))
                pl.when(ok_sr)(lambda: to_right(send_r).start())
                pl.when(ok_sl)(lambda: to_left(send_l).start())

            def finish():
                def took(copy, j, slot):
                    copy.wait_recv()
                    if not going_up:
                        self.combine(job, start + j * shard, place + slot * shard, shard, True)
                    elif last:
                        self.combine(job, start + j * shard, place + (n + 1 + j) * shard, shard, False)

                pl.when(ok_tr)(lambda: took(to_right(take_r), take_r, take_r))
                pl.when(ok_tl)(lambda: took(to_left(take_l), take_l, n if s == n - 2 else take_l))
                pl.when(ok_sr)(lambda: to_right(send_r).wait_send())
                pl.when(ok_sl)(lambda: to_left(send_l).wait_send())
                if not going_up and not last and s == n - 2:
                    pl.when(i <= n - 2)(lambda: self.signal(job, y, right))
                    pl.when(i >= 1)(lambda: self.signal(job, y + 1, left))

            return begin, finish

        return start + i * shard, shard, [op(s, False) for s in range(n - 1)], [op(s, True) for s in range(n - 1)]

    def peer_block(self, o):
        return pltpu.make_async_remote_copy(
            self.G.at[BLOCKS + o % 2],
            self.peer_buf.at[o],
            self.peer_send.at[o],
            self.peer_recv.at[o],
            device_id={"section": 1 - self.sec},
            device_id_type=MESH,
        )

    def fetch(self, o):
        return pltpu.make_async_copy(self.peer_buf.at[o], self.ST, self.load.at[0])

    def result(self, o, remote):
        dst = self.outs.at[o % OWN * 2 + self.sec]
        if remote:
            return pltpu.make_async_remote_copy(
                self.G.at[o],
                dst,
                self.out.at[o],
                self.out_recv.at[o],
                device_id={"section": 1 - self.sec},
                device_id_type=MESH,
            )
        return pltpu.make_async_copy(self.G.at[o], dst, self.out.at[o])

    def output(self, o):
        layer = 1 - o // OWN
        pl.when(layer == self.sec)(lambda: self.result(o, False).start())
        pl.when(layer != self.sec)(lambda: self.result(o, True).start())

    def wait_output(self, o):
        layer = 1 - o // OWN

        @pl.when(layer == self.sec)
        def _():
            self.result(o, False).wait()
            self.result(o, True).wait_recv()

        @pl.when(layer != self.sec)
        def _():
            self.result(o, True).wait_send()

    def step(self, o, k):
        if k == 0:
            self.peer_block(o).wait_recv()
            self.fetch(o).start()
            return
        if k == 1:
            self.fetch(o).wait()

            def body(i, _):
                rows = pl.ds(pl.multiple_of(i % 4 * 192, 96), 192)
                third = i // 4
                self.G[o, third, rows, :] = self.G[o, third, rows, :] + self.ST[third, rows, :]
                return 0

            lax.fori_loop(0, 12, body, 0)

        def advance(kind, typ):
            ops = self.plan((o, typ), kind, typ)
            if k >= 2:
                ops[k - 2][1]()
            if k - 1 < len(ops):
                ops[k - 1][0]()

        advance(0, jnp.int32(0))

        def rest(typ, _):
            advance(1, typ)
            return 0

        lax.fori_loop(1, 3, rest, 0)
        if k == self.steps - 1:
            self.output(o)

    def slot(self, t):
        for k in reversed(range(self.steps)):
            times = [row[k] for row in self.table]
            words = []
            for w in range(times[-1] // 31 + 1):
                words.append(sum(1 << (time - 31 * w) for time in times if 0 <= time - 31 * w < 31))
            word = jnp.int32(words[-1])
            for w in reversed(range(len(words) - 1)):
                word = jnp.where(t < 31 * (w + 1), jnp.int32(words[w]), word)

            @pl.when(((word >> (t % 31)) & 1 == 1) & (t <= times[-1]))
            def _(k=k, times=times):
                o = jnp.int32(0)
                for time in times[:-1]:
                    o = o + jnp.where(t > time, 1, 0)
                self.step(o, k)


    @property
    def slots(self):
        return self.table[-1][-1] + 1


def backward_kernel(
    dp_size, rep_size,
    cot, segs, wall, xs, qkvs, lses, atts, n1s, nbs, us, n2s, rss, tabs, biases, smalls,
    blocks, grad_small, ing, peer_buf,
    G, RB, ST, WR, UP, N2, NB, DB, DJ, N1, ATT, QK, U, DAT, DN, TAB, BIAS, RS, LSE, SM, SG, SB, SP,
    wsem, lsem, usem, send, recv, load, out, out_recv, peer_send, peer_recv, gsem, ssend, srecv, sync,
):
    sec = lax.axis_index("section")
    dp = lax.axis_index("dp")
    rep = lax.axis_index("rep")
    peer = {"section": 1 - sec}
    tokens = UP.shape[0]
    sums = Blocks(
        G, RB, ST, peer_buf, blocks,
        (send, recv, load, out, out_recv, peer_recv, peer_send, sync), dp, rep, dp_size, rep_size,
    )

    def weight(seq):
        layer, b = 1 - seq // BLOCKS, seq % BLOCKS
        return pltpu.make_async_copy(wall.at[layer, b], WR.at[b % 4], wsem.at[b % 4])

    def u_copy(layer, f):
        return pltpu.make_async_copy(us.at[layer, f], U.at[f % 2], usem.at[f % 2])

    def loads(layer):
        return (
            pltpu.make_async_copy(n2s.at[layer], N2, lsem.at[0]),
            pltpu.make_async_copy(nbs.at[layer], NB, lsem.at[1]),
            pltpu.make_async_copy(n1s.at[layer], N1, lsem.at[2]),
            pltpu.make_async_copy(atts.at[layer], ATT, lsem.at[3]),
            pltpu.make_async_copy(qkvs.at[layer], QK, lsem.at[4]),
            pltpu.make_async_copy(rss.at[layer], RS, lsem.at[5]),
            pltpu.make_async_copy(lses.at[layer], LSE, lsem.at[6]),
            pltpu.make_async_copy(xs.at[layer], N2, lsem.at[7]),
        )

    first = (
        pltpu.make_async_copy(cot.at[sec], UP, lsem.at[8]),
        pltpu.make_async_copy(smalls, SM, lsem.at[9]),
        pltpu.make_async_copy(tabs, TAB, lsem.at[10]),
        pltpu.make_async_copy(biases, BIAS, lsem.at[11]),
    )
    for copy in first:
        copy.start()

    barrier = pltpu.get_barrier_semaphore()
    partners = [(peer, None)]
    partners += [({"rep": rep ^ (1 << b)}, None) for b in range(rep_size.bit_length() - 1)]
    partners += [({"dp": dp ^ (1 << b)}, None) for b in range(dp_size.bit_length() - 1)]
    if sums.line:
        partners += [({"dp": jnp.minimum(dp + 1, dp_size - 1)}, dp < dp_size - 1)]
        partners += [({"dp": jnp.maximum(dp - 1, 0)}, dp > 0)]
    count = 0
    for device, valid in partners:

        def greet(device=device):
            pl.semaphore_signal(barrier, inc=1, device_id=device, device_id_type=MESH)

        if valid is None:
            greet()
            count = count + 1
        else:
            pl.when(valid)(greet)
            count = count + jnp.where(valid, 1, 0)
    pl.semaphore_wait(barrier, count)

    for seq in range(4):
        weight(seq).start()
    real = jnp.where(own_segments(segs, sec)[1] < SLOT // MINLEN, 1.0, 0.0).astype(F32)

    def in_copies(layer):
        mine = pltpu.make_async_copy(UP, ing.at[sec], gsem.at[0])
        theirs = pltpu.make_async_remote_copy(
            UP, ing.at[sec], gsem.at[1], gsem.at[2], device_id=peer, device_id_type=MESH
        )
        return mine, theirs

    def layer_step(li, _):
        layer = 1 - li
        copies = loads(layer)
        for copy in copies[:7]:
            copy.start()
        u_copy(layer, 0).start()
        u_copy(layer, 1).start()

        def slot(s):
            sums.slot(li * CALLS + s)

        def outer(lhs, rhs, b):
            o = li * OWN + b // 2
            mine = b % 2 == sec

            @pl.when(~mine & (o >= 2))
            def _():
                sums.peer_block(o - 2).wait_send()

            t = jnp.where(mine, o, BLOCKS + o % 2)
            for c in range(3):
                cols = slice(c * 256, (c + 1) * 256)
                G[t, c] = dot_tn(lhs[...], rhs[:, cols]).astype(BF16)

            pl.when(~mine)(lambda: sums.peer_block(o).start())

        @pl.when(li == 0)
        def _():
            for copy in first:
                copy.wait()
            UP[...] = (UP[...].astype(F32) * real).astype(BF16)

        copies[0].wait()
        copies[5].wait()

        def norm_back(grad, n, gain, scale):
            a = grad * gain
            m1 = jnp.mean(a, axis=1, keepdims=True)
            m2 = jnp.mean(a * n, axis=1, keepdims=True)
            return (a - m1 - n * m2) * scale

        def rows_sum(value):
            return jnp.sum(value, axis=0, keepdims=True)

        for row in (G_FFN, B_FFN, B_DOWN, G_ATTN, B_ATTN, B_OUT):
            SG[layer, row] = jnp.zeros((1, D), F32)
        for row in (13, 14, 15):
            SG[layer, row] = jnp.zeros((1, D), F32)

        def second_norm(c, _):
            rows = pl.ds(pl.multiple_of(c * 256, 256), 256)
            up = UP[rows, :].astype(F32)
            n = N2[rows, :].astype(F32)
            scale = RS[1, rows, 0:1]
            g = norm_back(up, n, SM[layer, G_FFN], scale)
            DN[rows, :] = g
            DB[rows, :] = g.astype(BF16)
            SG[layer, G_FFN] += rows_sum(up * n)
            SG[layer, B_FFN] += rows_sum(up)
            SG[layer, B_DOWN] += rows_sum(g)
            return 0

        lax.fori_loop(0, tokens // 256, second_norm, 0)
        copies[7].start()
        copies[1].wait()

        def ffn(f, _):
            u_copy(layer, f).wait()
            weight(li * BLOCKS + 2 * f).wait()
            weight(li * BLOCKS + 2 * f + 1).wait()
            down, up = WR.at[2 * f % 4], WR.at[(2 * f + 1) % 4]
            for c in range(3):
                cols = slice(c * 256, (c + 1) * 256)
                u = U[f % 2, :, cols].astype(F32)
                square, t = gelu_parts(u)
                lift = 1.0 + t
                DJ[1, :, cols] = (0.5 * u * lift).astype(BF16)
                slope = 0.5 * lift * (1.0 + u * (1.0 - t) * (GELU_A * (1.0 + 3.0 * GELU_B * square)))
                grad = dot_t(DB[...], down[cols, :]) * slope
                SG[layer, B_IN + f, :, cols] = rows_sum(grad)
                DJ[0, :, cols] = grad.astype(BF16)
            outer(DJ.at[1], DB, 2 * f)
            slot(2 * f)
            outer(NB, DJ.at[0], 2 * f + 1)
            for c in range(3):
                cols = slice(c * 256, (c + 1) * 256)
                DN[:, cols] += dot_t(DJ[0], up[cols, :])
            weight(li * BLOCKS + 2 * f + 4).start()
            weight(li * BLOCKS + 2 * f + 5).start()
            pl.when(f + 2 < CHUNKS)(lambda: u_copy(layer, f + 2).start())
            slot(2 * f + 1)
            return 0

        lax.fori_loop(0, CHUNKS, ffn, 0)
        copies[2].wait()

        def first_norm(c, _):
            rows = pl.ds(pl.multiple_of(c * 256, 256), 256)
            up = DN[rows, :]
            n = N1[rows, :].astype(F32)
            g = norm_back(up, n, SM[layer, G_ATTN], RS[0, rows, 0:1])
            DN[rows, :] = g
            DB[rows, :] = g.astype(BF16)
            SG[layer, G_ATTN] += rows_sum(up * n)
            SG[layer, B_ATTN] += rows_sum(up)
            SG[layer, B_OUT] += rows_sum(g)
            return 0

        lax.fori_loop(0, tokens // 256, first_norm, 0)
        copies[3].wait()
        outer(ATT, DB, OUT)
        weight(li * BLOCKS + OUT).wait()
        w_out = WR.at[OUT % 4]
        for c in range(3):
            cols = slice(c * 256, (c + 1) * 256)
            DAT[:, cols] = dot_t(DB[...], w_out[cols, :]).astype(BF16)
        pl.when(li == 0)(lambda: weight(BLOCKS).start())
        slot(2 * CHUNKS)
        copies[4].wait()
        copies[6].wait()

        def pair(hp, _):
            lanes = pl.ds(pl.multiple_of(hp * 128, 128), 128)
            q2 = QK[0, :, lanes]
            k2 = QK[1, :, lanes]
            v2 = QK[2, :, lanes]
            o2 = DAT[:, lanes]
            low = low_lanes(k2.shape)
            k_t = k2.T
            zero = jnp.zeros_like(k2)
            grads_q, grads_k, grads_v = [], [], []
            for h in range(2):
                mask = low if h == 0 else ~low
                s = dot_t(jnp.where(mask, k2, zero), q2) * SCORE + BIAS[...]
                p = jnp.exp2(s - LSE[hp, h : h + 1, :])
                dprob = dot_t(jnp.where(mask, v2, zero), o2)
                inner = jnp.sum(p * dprob, axis=0, keepdims=True)
                ds = (p * (dprob - inner)).astype(BF16)
                grads_v.append(dot(p.astype(BF16), o2))
                grads_k.append(dot(ds, q2))
                grads_q.append(dot(k_t[h * HEAD : (h + 1) * HEAD], ds))
            scale = 1.0 / math.sqrt(HEAD)
            gq = jnp.concatenate(grads_q, axis=0).T * scale
            gk = jnp.where(low, grads_k[0], grads_k[1]) * scale
            gv = jnp.where(low, grads_v[0], grads_v[1])
            cos, sin = TAB[0], TAB[1]
            gq = gq * cos - swap_halves(gq) * sin
            gk = gk * cos - swap_halves(gk) * sin
            for third, g in enumerate((gq, gk, gv)):
                DJ[third, :, lanes] = g.astype(BF16)
                SG[layer, B_QKV + third, :, lanes] = rows_sum(g)
            slot(2 * CHUNKS + 1 + hp)
            return 0

        lax.fori_loop(0, PAIRS, pair, 0)
        copies[7].wait()

        def third_step(third, _):
            outer(N2, DJ.at[third], QKV + third)
            weight(li * BLOCKS + QKV + third).wait()
            w = WR.at[(QKV + third) % 4]
            for c in range(3):
                cols = slice(c * 256, (c + 1) * 256)
                DN[:, cols] += dot_t(DJ[third], w[cols, :])
            pl.when(li == 0)(lambda: weight(BLOCKS + 1 + third).start())
            slot(CALLS - 3 + third)
            return 0

        lax.fori_loop(0, 3, third_step, 0)

        mine, theirs = in_copies(layer)
        @pl.when(li == 1)
        def _():
            pl.when(sec == 1)(lambda: mine.wait())
            pl.when(sec == 0)(lambda: theirs.wait_send())

        UP[...] = DN[...].astype(BF16)
        pl.when(layer == sec)(lambda: mine.start())
        pl.when(layer != sec)(lambda: theirs.start())
        return 0

    lax.fori_loop(0, 2, layer_step, 0)

    small_partners = [peer] + [device for device, valid in partners[1:] if valid is None]

    def small_copy(m):
        src = SG.at[1 - sec] if m == 0 else SP.at[m - 1]
        return pltpu.make_async_remote_copy(
            src, SB.at[m], ssend.at[m], srecv.at[m], device_id=small_partners[m], device_id_type=MESH
        )

    small_copy(0).start()

    def small_step(m):
        small_copy(m).wait_recv()
        SP[m] = (SG[sec] if m == 0 else SP[m - 1]) + SB[m]
        if m + 1 < len(small_partners):
            small_copy(m + 1).start()

    rounds = max(sums.slots - 2 * CALLS, len(small_partners))

    def final(i, _):
        sums.slot(2 * CALLS + i)
        for m in range(len(small_partners)):
            pl.when(i == m)(functools.partial(small_step, m))
        return 0

    lax.fori_loop(0, rounds, final, 0)
    for m in range(len(small_partners)):
        small_copy(m).wait_send()
    small_out = pltpu.make_async_copy(SP.at[len(small_partners) - 1], grad_small, ssend.at[0])
    small_out.start()

    for o in (BLOCKS - 2, BLOCKS - 1):
        sums.peer_block(o).wait_send()

    def out_wait(o, _):
        sums.wait_output(o)
        return 0

    lax.fori_loop(0, BLOCKS, out_wait, 0)
    small_out.wait()
    mine, theirs = in_copies(0)
    pl.when(sec == 0)(lambda: mine.wait())
    pl.when(sec == 1)(lambda: theirs.wait_send())
    theirs.wait_recv()


RING = 6


def convert_kernel(
    blocks, small,
    out_q, out_o, out_i, out_d, b_q, b_o, g_a, b_a, b_i, b_d, g_f, b_f,
    LOW, HIGH, isem, osem,
):
    tiles = []
    for b in range(BLOCKS):
        for c in range(3):
            cols = pl.ds(c * THIRD, THIRD)
            if b < OUT and b % 2 == 0:
                dst = out_d.at[0, pl.ds(b // 2 * D, D), cols]
            elif b < OUT:
                dst = out_i.at[0, :, pl.ds(b // 2 * D + c * THIRD, THIRD)]
            elif b == OUT:
                dst = out_o.at[0, :, cols]
            else:
                dst = out_q.at[0, :, pl.ds((b - QKV) * D + c * THIRD, THIRD)]
            tiles.append((blocks.at[b, c], dst))
    reads = [pltpu.make_async_copy(src, LOW.at[i % RING], isem.at[i % RING]) for i, (src, _) in enumerate(tiles)]
    writes = [pltpu.make_async_copy(HIGH.at[i % RING], dst, osem.at[i % RING]) for i, (_, dst) in enumerate(tiles)]
    for i in range(RING):
        reads[i].start()
    for row, ref in ((B_QKV, b_q), (B_OUT, b_o), (G_ATTN, g_a), (B_ATTN, b_a), (B_IN, b_i), (B_DOWN, b_d), (G_FFN, g_f), (B_FFN, b_f)):
        for i in range(ref.shape[1] // D):
            ref[0:1, i * D : (i + 1) * D] = small[row + i]
    for i in range(len(tiles)):
        reads[i].wait()
        if i >= RING:
            writes[i - RING].wait()

        def body(r, _, at=i % RING):
            rows = pl.ds(pl.multiple_of(r * 192, 64), 192)
            HIGH[at, rows, :] = LOW[at, rows, :].astype(F32)
            return 0

        lax.fori_loop(0, 4, body, 0)
        writes[i].start()
        if i + RING < len(tiles):
            reads[i + RING].start()
    for write in writes[len(tiles) - RING :]:
        write.wait()


def per_device(
    dp_size, rep_size, inputs, segments, cotangent, w_qkv, b_qkv, w_out, b_out, g_attn, b_attn, w_in, b_in, w_down,
    b_down, g_ffn, b_ffn,
):
    tokens = inputs.shape[1]
    anywhere = pl.BlockSpec(memory_space=pl.ANY)
    in_vmem = pl.BlockSpec(memory_space=pltpu.VMEM)

    def shape(*dims, dtype=BF16):
        return jax.ShapeDtypeStruct(dims, dtype)

    def mem(*dims, dtype=BF16):
        return pltpu.VMEM(dims, dtype)

    dma = pltpu.SemaphoreType.DMA
    stash = pl.pallas_call(
        forward_kernel,
        out_shape=(
            shape(2, BLOCKS, D, D),
            shape(2, tokens, D),
            shape(2, 3, tokens, D),
            shape(2, PAIRS, 8, tokens, dtype=F32),
            shape(2, tokens, D),
            shape(2, tokens, D),
            shape(2, tokens, D),
            shape(2, CHUNKS, tokens, D),
            shape(2, tokens, D),
            shape(2, 2, tokens, 128, dtype=F32),
            shape(2, tokens, 128, dtype=F32),
            shape(tokens, tokens, dtype=F32),
            shape(2, tokens, D),
            shape(2, SMALL, 1, D, dtype=F32),
        ),
        in_specs=[anywhere, in_vmem] + [anywhere] * 4 + [in_vmem] * 8,
        out_specs=(anywhere,) * 14,
        scratch_shapes=[
            mem(2, BLOCKS, D, D),
            mem(2, SMALL, 1, D, dtype=F32),
            mem(3, tokens, D),
            mem(2, 3, tokens, D),
            mem(2, PAIRS, 8, tokens, dtype=F32),
            mem(2, tokens, D),
            mem(2, tokens, D),
            mem(2, tokens, D),
            mem(2, CHUNKS, tokens, D),
            mem(2, tokens, D),
            mem(2, 2, tokens, 128, dtype=F32),
            mem(2, tokens, 128, dtype=F32),
            mem(tokens, tokens, dtype=F32),
            mem(tokens, D, dtype=F32),
            mem(tokens, D),
            dma((BLOCKS,)),
            dma((BLOCKS,)),
            dma((BLOCKS,)),
            dma((6,)),
            dma((2, BLOCKS)),
            dma((2, 9)),
            dma((3,)),
        ],
        compiler_params=pltpu.CompilerParams(collective_id=0, has_side_effects=True, vmem_limit_bytes=VMEM_LIMIT),
        name="forward",
    )(inputs, segments, w_qkv, w_out, w_in, w_down, b_qkv, b_out, g_attn, b_attn, b_in, b_down, g_ffn, b_ffn)
    (wall, xs, qkvs, lses, atts, n1s, nbs, us, n2s, rss, tabs, biases, acts, smalls) = stash

    line = dp_size == 4 and rep_size == 4
    bits = dp_size.bit_length() + rep_size.bit_length() - 2
    ring = BLOCKS
    landing = 1152 if line else 912
    out = pl.pallas_call(
        functools.partial(backward_kernel, dp_size, rep_size),
        out_shape=(
            shape(BLOCKS, 3, D, THIRD),
            shape(SMALL, 1, D, dtype=F32),
            shape(2, tokens, D),
            shape(BLOCKS, 3, D, THIRD),
        ),
        in_specs=[anywhere, in_vmem] + [anywhere] * 13,
        out_specs=(anywhere,) * 4,
        scratch_shapes=[
            mem(BLOCKS + 2, 3, D, THIRD),
            mem(ring, 3, landing, THIRD),
            mem(3, D, THIRD),
            mem(4, D, D),
            mem(tokens, D),
            mem(tokens, D),
            mem(tokens, D),
            mem(tokens, D),
            mem(3, tokens, D),
            mem(tokens, D),
            mem(tokens, D),
            mem(3, tokens, D),
            mem(2, tokens, D),
            mem(tokens, D),
            mem(tokens, D, dtype=F32),
            mem(2, tokens, 128, dtype=F32),
            mem(tokens, tokens, dtype=F32),
            mem(2, tokens, 128, dtype=F32),
            mem(PAIRS, 8, tokens, dtype=F32),
            mem(2, SMALL, 1, D, dtype=F32),
            mem(2, SMALL, 1, D, dtype=F32),
            mem(bits + 1, SMALL, 1, D, dtype=F32),
            mem(bits + 1, SMALL, 1, D, dtype=F32),
            dma((4,)),
            dma((12,)),
            dma((2,)),
            dma((3 * ring, 2)),
            dma((3 * ring, 10)),
            dma((1,)),
            dma((BLOCKS,)),
            dma((BLOCKS,)),
            dma((BLOCKS,)),
            dma((BLOCKS,)),
            dma((3,)),
            dma((bits + 1,)),
            dma((bits + 1,)),
            pltpu.SemaphoreType.REGULAR((3 * ring, 3)),
        ],
        compiler_params=pltpu.CompilerParams(collective_id=1, has_side_effects=True, vmem_limit_bytes=VMEM_LIMIT),
        name="backward",
    )(cotangent, segments, wall, xs, qkvs, lses, atts, n1s, nbs, us, n2s, rss, tabs, biases, smalls)
    blocks, grad_small, ing, _ = out
    vectors = (3 * D, D, D, D, CHUNKS * D, D, D, D)
    grads = pl.pallas_call(
        convert_kernel,
        out_shape=(
            *(shape(1, *dims, dtype=F32) for dims in ((D, 3 * D), (D, D), (D, CHUNKS * D), (CHUNKS * D, D))),
            *(shape(1, size, dtype=F32) for size in vectors),
        ),
        in_specs=[anywhere, in_vmem],
        out_specs=(anywhere,) * 4 + (in_vmem,) * 8,
        scratch_shapes=[
            mem(RING, D, THIRD),
            mem(RING, D, THIRD, dtype=F32),
            dma((RING,)),
            dma((RING,)),
        ],
        compiler_params=pltpu.CompilerParams(vmem_limit_bytes=VMEM_LIMIT),
        name="convert",
    )(blocks, grad_small)
    grad_q, grad_o, grad_i, grad_d, b_q, b_o, g_a, b_a, b_i, b_d, g_f, b_f = grads
    return acts[None], ing[None], grad_q, b_q, grad_o, b_o, g_a, b_a, grad_i, b_i, grad_d, b_d, g_f, b_f


def solution(mesh):
    tokens = ("dp", "rep")
    weight, vector = P("section", None, None), P("section", None)
    weights = (weight, vector, weight, vector, vector, vector, weight, vector, weight, vector, vector, vector)
    activations = P("section", None, tokens, None)
    return jax.shard_map(
        functools.partial(per_device, mesh.shape["dp"], mesh.shape["rep"]),
        mesh=mesh,
        in_specs=(P(None, tokens, None), P(None, tokens), P(None, tokens, None), *weights),
        out_specs=(activations, activations, *weights),
        check_vma=False,
    )
```
